32 devices in a mesh: dp: 4 (over x, core), space: 8 (over z, y).
Axes of the slice: x: 2, y: 2, z: 4, core: 2. Of those that a mesh axis runs over, the one named last changes fastest.
Arguments:
- acts_in: bfloat16 [4, 32, 64, 32, 128], P('dp', 'space'), may hold values from -6 to 6
- pre_act: bfloat16 [4, 32, 64, 32, 128], P('dp', 'space'), may hold values from -6 to 6
- weight_two: bfloat16 [128, 3, 3, 3, 128], P('space'), may hold values from -0.109375 to 0.109375
- grad_out: bfloat16 [4, 16, 32, 16, 128], P('dp', None, None, None, 'space'), may hold values from -6 to 6
Outputs:
- fine_grad: float32 [128, 3, 3, 3, 128], P('space')
- coarse_grad: float32 [128, 3, 3, 3, 128], P('space')
The draws below stay inside these ranges and needn't reach their ends.
All inputs are finite; a program needn't handle non-finite values.
Results may differ from the reference program's by a relative error of at most 0.003.
Values may be sent and summed in bfloat16 or wider, within the bound.
A program may use at most 128 MiB of HBM per device.

```python
import math
import jax
import jax.numpy as jnp
from jax import lax

C = 128
NY = 64
NZ = 32
SAMPLES = 4
NX = 32


def raised(result, key, source, target, shards_of, factor):
    def block_of(position):
        return (jnp.arange(result.shape[position]) // (result.shape[position] // shards_of)).reshape((-1,) + (1,) * (result.ndim - 1 - position))

    near = jax.random.permutation(key, shards_of)[block_of(target)]
    far = (block_of(target) + shards_of // 2) % shards_of
    return jnp.where((block_of(source) == near) | (block_of(source) == far), factor * result, result)


def level_of(stream_key, extent, split, least, top_value):
    factor_of = 1.0
    for dim, blocks in split:
        draws = jax.random.uniform(jax.random.fold_in(jax.random.fold_in(stream_key, 6), dim), (blocks,), jnp.float32, least / len(split), top_value / len(split))
        factor_of = factor_of * jnp.repeat(jnp.exp(draws), extent[dim] // blocks).reshape((-1,) + (1,) * (len(extent) - 1 - dim))
    return factor_of


def noise(own_key, extent, deviation, bound, cuts=(), held_as=jnp.bfloat16):
    gain = level_of(own_key, extent, cuts, -0.22, 0.18) if cuts else 1.0
    array = jax.random.normal(own_key, extent, jnp.float32) * deviation * gain
    return jnp.minimum(jnp.maximum(array, -bound), bound).astype(held_as)


def heavy_noise(own_key, dims, deviation, bound, cuts, heavy, kind=jnp.bfloat16):
    drawn = deviation * jax.random.normal(own_key, dims, jnp.float32)
    if cuts:
        drawn = drawn * level_of(own_key, dims, cuts, -0.22, 0.18)
    return jnp.clip(raised(drawn, jax.random.fold_in(own_key, 3), *heavy), -bound, bound).astype(kind)


def setup_inputs(seed: int = 0) -> dict:
    seeds = jax.random.split(jax.random.key(seed), 5)
    return {
        "acts_in": noise(seeds[0], (SAMPLES, NX, NY, NZ, C), 1.0, 6.0, ((0, 4), (1, 8))),
        "pre_act": heavy_noise(seeds[1], (SAMPLES, NX, NY, NZ, C), 1.0, 6.0, ((0, 4), (1, 8)), (1, 4, 8, 2.0)),
        "weight_two": noise(seeds[2], (C, 3, 3, 3, C), (27 * C) ** -0.5, 0.109375, ((0, 8),)),
        "grad_out": noise(seeds[3], (SAMPLES, NX // 2, NY // 2, NZ // 2, C), 1.0, 6.0, ((0, 4), (4, 8))),
    }


leak_slope = 0.3
parity_taps = {0: ((1, 0),), 1: ((0, 1), (2, 0))}

def transpose_conv(padded, weight):
    rows_x = padded.shape[0] - 1
    rows_y = padded.shape[1] - 1
    rows_z = padded.shape[2] - 1
    classes = []
    for parity_x in (0, 1):
        for parity_y in (0, 1):
            for parity_z in (0, 1):
                pieces = []
                blocks = []
                for tap_x, move_x in parity_taps[parity_x]:
                    for tap_y, move_y in parity_taps[parity_y]:
                        for tap_z, move_z in parity_taps[parity_z]:
                            pieces.append(padded[move_x:move_x + rows_x, move_y:move_y + rows_y, move_z:move_z + rows_z, :])
                            blocks.append(weight[:, tap_x, tap_y, tap_z, :])
                stacked = jnp.concatenate(pieces, axis=3)
                flat = stacked.reshape(-1, stacked.shape[3])
                mixing = jnp.concatenate(blocks, axis=0)
                classes.append(jnp.dot(flat, mixing, preferred_element_type=jnp.float32))
    outputs = weight.shape[4]
    joined = jnp.stack(classes).reshape(2, 2, 2, rows_x, rows_y, rows_z, outputs)
    joined = joined.transpose(3, 0, 4, 1, 5, 2, 6)
    return joined.reshape(2 * rows_x, 2 * rows_y, 2 * rows_z, outputs)

def weight_terms(source, gradient, stride):
    count_x, count_y, count_z, filters = gradient.shape
    flat_grad = gradient.reshape(-1, filters)
    terms = []
    for tap_x in range(3):
        for tap_y in range(3):
            for tap_z in range(3):
                piece = source[tap_x:tap_x + stride * count_x:stride, tap_y:tap_y + stride * count_y:stride, tap_z:tap_z + stride * count_z:stride, :]
                terms.append(lax.dot_general(flat_grad, piece.reshape(-1, piece.shape[3]), (((0,), (0,)), ((), ())), preferred_element_type=jnp.float32))
    return jnp.stack(terms, axis=1).reshape(filters, 3, 3, 3, source.shape[3])

def reference(acts_in, pre_act, weight_two, grad_out):
    scaling = 1.0 / math.sqrt(SAMPLES * NX * NY * NZ)

    def sample_step(carry, items):
        acts, before, cotangent = items
        before_f = before.astype(jnp.float32)
        hidden = jnp.where(before_f > 0, before_f, leak_slope * before_f).astype(jnp.bfloat16)
        lower = jnp.pad(hidden, ((1, 0), (1, 0), (1, 0), (0, 0)))
        coarse = weight_terms(lower, cotangent, 2)
        upper = jnp.pad(cotangent, ((0, 1), (0, 1), (0, 1), (0, 0)))
        back = transpose_conv(upper, weight_two)
        delta = (back * jnp.where(before_f > 0, 1.0, leak_slope)).astype(jnp.bfloat16)
        framed = jnp.pad(acts, ((1, 1), (1, 1), (1, 1), (0, 0)))
        fine = weight_terms(framed, delta, 1)
        return ((carry[0] + fine, carry[1] + coarse), None)
    zeros = jnp.zeros((C, 3, 3, 3, C), jnp.float32)
    totals, unused = lax.scan(sample_step, (zeros, zeros), (acts_in, pre_act, grad_out))
    return (totals[0] * scaling, totals[1] * scaling)
```

```python
import functools
import math

import jax
import jax.numpy as jnp
from jax import lax
from jax.experimental import pallas as pl
from jax.experimental.pallas import tpu as pltpu
from jax.sharding import PartitionSpec as P

leak_slope = 0.3
parity_taps = {0: ((1, 0),), 1: ((0, 1), (2, 0))}
MESH = pl.DeviceIdType.MESH
VMEM = pltpu.VMEM


def passed_along(block, axis, distance):
    devices = range(lax.axis_size(axis))
    route = [(i - distance, i) for i in devices if i - distance in devices]
    return lax.ppermute(block, axis, route)


def padded_2(shard, sides, width):
    for axis, dim in sides:
        size, length = (lax.axis_size(axis), shard.shape[dim])
        up = [(i, (i + 1) % size) for i in range(size - 1)]
        down = [(j, i) for i, j in up]
        last = lax.slice_in_dim(shard, length - width, length, axis=dim)
        initial = lax.slice_in_dim(shard, 0, width, axis=dim)
        before = lax.ppermute(last, axis, up)
        after = lax.ppermute(initial, axis, down)
        shard = jnp.concatenate([before, shard, after], axis=dim)
    return shard


def remote(src, dst, send, recv, target):
    return pltpu.make_async_remote_copy(
        src_ref=src,
        dst_ref=dst,
        send_sem=send,
        recv_sem=recv,
        device_id=target,
        device_id_type=MESH,
    )


def greet(dp, parts, whole_dp):
    me, mine = lax.axis_index("space"), lax.axis_index("dp")
    barrier = pltpu.get_barrier_semaphore()
    count = 0
    for d in range(1, parts):
        pl.semaphore_signal(
            barrier, inc=1, device_id={"space": lax.rem(me + d, parts)}, device_id_type=MESH
        )
        count += 1
    if whole_dp:
        for d in range(1, dp):
            pl.semaphore_signal(
                barrier, inc=1, device_id={"dp": lax.rem(mine + d, dp)}, device_id_type=MESH
            )
            count += 1
    else:
        pl.semaphore_signal(
            barrier, inc=1, device_id={"dp": mine + 1 - 2 * lax.rem(mine, 2)}, device_id_type=MESH
        )
        count += 1
    pl.semaphore_wait(barrier, count)


def gather_kernel(dp, parts, w_ref, g_ref, w_out, g_out, wbuf, gbuf, sends, recvs):
    me, mine = lax.axis_index("space"), lax.axis_index("dp")
    core = lax.rem(mine, 2)
    partner = mine + 1 - 2 * core
    half = w_ref.shape[0] // 2
    greet(dp, parts, False)
    gcopies, wcopies, forwards = [], [], []
    for d in range(1, parts):
        t = lax.rem(me + d, parts)
        copy = remote(
            g_ref.at[t], gbuf.at[d - 1], sends.at[0, d - 1], recvs.at[0, d - 1], {"space": t}
        )
        copy.start()
        gcopies.append(copy)
    own = w_ref.at[pl.ds(pl.multiple_of(core * half, 16), half)]
    for d in range(1, parts):
        t = lax.rem(me + d, parts)
        copy = remote(
            own, wbuf.at[d - 1, core], sends.at[1, d - 1], recvs.at[1, d - 1], {"space": t}
        )
        copy.start()
        wcopies.append(copy)
    g_out[me] = g_ref[me]
    w_out[me] = w_ref[...]
    for d in range(1, parts):
        wcopies[d - 1].wait_recv()
        copy = remote(
            wbuf.at[d - 1, core],
            wbuf.at[d - 1, core],
            sends.at[2, d - 1],
            recvs.at[2, d - 1],
            {"dp": partner},
        )
        copy.start()
        forwards.append(copy)
    for d in range(1, parts):
        s = lax.rem(me + parts - d, parts)
        gcopies[d - 1].wait_recv()
        g_out[s] = gbuf[d - 1]
    for d in range(1, parts):
        s = lax.rem(me + parts - d, parts)
        forwards[d - 1].wait_recv()
        w_out[s, pl.ds(0, half)] = wbuf[d - 1, 0]
        w_out[s, pl.ds(half, half)] = wbuf[d - 1, 1]
    for copy in gcopies + wcopies + forwards:
        copy.wait_send()


def gathered(dp, parts, w, g):
    half = w.shape[0] // 2
    return pl.pallas_call(
        functools.partial(gather_kernel, dp, parts),
        out_shape=[
            jax.ShapeDtypeStruct((parts,) + w.shape, w.dtype),
            jax.ShapeDtypeStruct(g.shape, g.dtype),
        ],
        in_specs=[pl.BlockSpec(memory_space=VMEM)] * 2,
        out_specs=[pl.BlockSpec(memory_space=VMEM)] * 2,
        scratch_shapes=[
            VMEM((parts - 1, 2, half, 128), w.dtype),
            VMEM((parts - 1,) + g.shape[1:], g.dtype),
            pltpu.SemaphoreType.DMA((3, parts - 1)),
            pltpu.SemaphoreType.DMA((3, parts - 1)),
        ],
        compiler_params=pltpu.CompilerParams(
            collective_id=0, has_side_effects=True, vmem_limit_bytes=32 << 20
        ),
    )(w, g)


def reduce_kernel(dp, parts, scaling, *refs):
    terms = refs[:18]
    out, part, got, away, came, apart, near, whole, sends, recvs = refs[18:]
    me, mine = lax.axis_index("space"), lax.axis_index("dp")
    core = lax.rem(mine, 2)
    rest = mine // 2
    ranks = dp // 2
    partner = mine + 1 - 2 * core
    chunk = part.shape[0] // dp
    half = chunk * ranks
    filters, inputs = part.shape[1:]
    rows = filters // parts
    for u in range(part.shape[0]):
        if u < 54:
            z = (u % 3) * inputs
            part[u] = terms[u // 3][:, z : z + inputs]
        else:
            part[u] = jnp.zeros((filters, inputs), jnp.float32)
    greet(dp, parts, True)
    first = []
    theirs = (1 - core) * half
    for d in list(range(1, ranks)) + [0]:
        j = lax.rem(rest + d, ranks)
        copy = remote(
            part.at[pl.ds(theirs + j * chunk, chunk)],
            got.at[d],
            sends.at[0, d],
            recvs.at[0, d],
            {"dp": partner},
        )
        copy.start()
        first.append(copy)
    second = []
    for d, copy in zip(list(range(1, ranks)) + [0], first):
        j = lax.rem(rest + d, ranks)
        base = core * half + j * chunk
        copy.wait_recv()
        if d:

            def fill(u, carry):
                away[d - 1, u] = (part[base + u] + got[d, u]).astype(jnp.bfloat16)
                return carry

            lax.fori_loop(0, chunk, fill, 0)
            onward = remote(
                away.at[d - 1],
                came.at[d - 1],
                sends.at[1, d],
                recvs.at[1, d],
                {"dp": 2 * j + core},
            )
            onward.start()
            second.append(onward)
    base = core * half + rest * chunk
    for onward in second:
        onward.wait_recv()

    def settle(u, carry):
        total = part[base + u] + got[0, u]
        for d in range(1, ranks):
            total = total + came[d - 1, u].astype(jnp.float32)
        got[0, u] = total
        return carry

    lax.fori_loop(0, chunk, settle, 0)
    third = []
    for d in range(1, parts):
        t = lax.rem(me + d, parts)
        start = pl.multiple_of(t * rows, rows)
        apart[d - 1] = (
            got[0, :, pl.ds(start, rows), :].reshape(chunk * rows, inputs).astype(jnp.bfloat16)
        )
        copy = remote(
            apart.at[d - 1], near.at[d - 1], sends.at[2, d], recvs.at[2, d], {"space": t}
        )
        copy.start()
        third.append(copy)
    start = pl.multiple_of(me * rows, rows)
    total = got[0, :, pl.ds(start, rows), :].reshape(chunk * rows, inputs)
    for d in range(1, parts):
        third[d - 1].wait_recv()
        total = total + near[d - 1].astype(jnp.float32)
    whole[0] = total * scaling
    fourth = []
    for d in range(1, dp):
        copy = remote(
            whole.at[0],
            whole.at[d],
            sends.at[3, d],
            recvs.at[3, d],
            {"dp": lax.rem(mine + d, dp)},
        )
        copy.start()
        fourth.append(copy)
    out[core * ranks + rest] = whole[0]
    for d in range(1, dp):
        fourth[d - 1].wait_recv()
        other = lax.rem(mine + dp - d, dp)
        out[lax.rem(other, 2) * ranks + other // 2] = whole[d]
    for copy in first + second + third + fourth:
        copy.wait_send()


def reduced(dp, parts, scaling, terms):
    filters, width = terms[0].shape
    inputs = width // 3
    chunk = -(-54 // dp)
    ranks = dp // 2
    rows = filters // parts
    most = max(dp, parts)
    f32, bf16 = jnp.float32, jnp.bfloat16
    return pl.pallas_call(
        functools.partial(reduce_kernel, dp, parts, scaling),
        out_shape=jax.ShapeDtypeStruct((dp, chunk * rows, inputs), f32),
        in_specs=[pl.BlockSpec(memory_space=VMEM)] * 18,
        out_specs=pl.BlockSpec(memory_space=VMEM),
        scratch_shapes=[
            VMEM((chunk * dp, filters, inputs), f32),
            VMEM((ranks, chunk, filters, inputs), f32),
            VMEM((ranks - 1, chunk, filters, inputs), bf16),
            VMEM((ranks - 1, chunk, filters, inputs), bf16),
            VMEM((parts - 1, chunk * rows, inputs), bf16),
            VMEM((parts - 1, chunk * rows, inputs), bf16),
            VMEM((dp, chunk * rows, inputs), f32),
            pltpu.SemaphoreType.DMA((4, most)),
            pltpu.SemaphoreType.DMA((4, most)),
        ],
        compiler_params=pltpu.CompilerParams(
            collective_id=1, has_side_effects=True, vmem_limit_bytes=48 << 20
        ),
    )(*terms)


def transpose_conv(padded, weight):
    rows_x = padded.shape[0] - 1
    rows_y = padded.shape[1] - 1
    rows_z = padded.shape[2] - 1
    outputs = weight.shape[2]
    zpair = jnp.concatenate([padded[:, :, :rows_z, :], padded[:, :, 1:, :]], axis=3)
    nothing = jnp.zeros(weight.shape[1:], weight.dtype)
    classes = []
    for parity_x in (0, 1):
        for parity_y in (0, 1):
            pieces = []
            blocks = []
            for tap_x, move_x in parity_taps[parity_x]:
                for tap_y, move_y in parity_taps[parity_y]:
                    pieces.append(zpair[move_x : move_x + rows_x, move_y : move_y + rows_y])
                    base = 9 * tap_x + 3 * tap_y
                    first = jnp.concatenate([weight[base + 1], weight[base + 2]], axis=1)
                    second = jnp.concatenate([nothing, weight[base]], axis=1)
                    blocks.append(jnp.concatenate([first, second], axis=0))
            stacked = jnp.concatenate(pieces, axis=3)
            flat = stacked.reshape(-1, stacked.shape[3])
            mixing = jnp.concatenate(blocks, axis=0)
            classes.append(jnp.dot(flat, mixing, preferred_element_type=jnp.float32))
    joined = jnp.stack(classes).reshape(2, 2, rows_x, rows_y, rows_z, 2 * outputs)
    joined = joined.transpose(2, 0, 3, 1, 4, 5)
    return joined.reshape(2 * rows_x, 2 * rows_y, 2 * rows_z, outputs)


def depth_taps(volume):
    count_x, count_y, count_z, channels = volume.shape
    paired = volume.reshape(count_x, count_y, count_z // 2, 2 * channels)
    even = paired[..., :channels]
    odd = paired[..., channels:]
    earlier = jnp.pad(odd[:, :, :-1, :], ((0, 0), (0, 0), (1, 0), (0, 0)))
    return jnp.concatenate([earlier, even, odd], axis=3)


def coarse_terms(hidden, below, gradient, sizes):
    count_x, count_y, count_z = sizes
    stacked = depth_taps(hidden)
    width = stacked.shape[3]
    split = stacked.reshape(count_x, 2, count_y, 2, count_z, width)
    rim = depth_taps(below).reshape(1, count_y, 2, count_z, width)
    by_x = [jnp.concatenate([rim, split[:-1, 1]], axis=0), split[:, 0], split[:, 1]]
    terms = []
    for tap_x in range(3):
        plane = by_x[tap_x]
        by_y = [
            jnp.pad(plane[:, :-1, 1], ((0, 0), (1, 0), (0, 0), (0, 0))),
            plane[:, :, 0],
            plane[:, :, 1],
        ]
        for tap_y in range(3):
            piece = by_y[tap_y].reshape(-1, width)
            terms.append(jnp.dot(gradient, piece, preferred_element_type=jnp.float32))
    return terms


def fine_terms(framed, gradient):
    count_x, count_y, count_z, filters = gradient.shape
    flat_grad = gradient.reshape(-1, filters)
    stacked = jnp.concatenate(
        [framed[:, :, shift : shift + count_z, :] for shift in range(3)], axis=3
    )
    width = stacked.shape[3]
    terms = []
    for tap_x in range(3):
        for tap_y in range(3):
            piece = stacked[tap_x : tap_x + count_x, tap_y : tap_y + count_y].reshape(-1, width)
            terms.append(
                lax.dot_general(
                    flat_grad, piece, (((0,), (0,)), ((), ())), preferred_element_type=jnp.float32
                )
            )
    return terms


def body(acts_in, pre_act, weight_two, grad_out):
    parts = lax.axis_size("space")
    groups = lax.axis_size("dp")
    acts = acts_in[0]
    depth, across, height, channels = acts.shape
    rows = weight_two.shape[0]
    filters = rows * parts
    scaling = 1.0 / math.sqrt(groups * depth * parts * across * height)
    half_x, half_y, half_z = depth // 2, across // 2, height // 2
    plane = half_y * half_z
    before_f = pre_act[0].astype(jnp.float32)
    hidden = jnp.where(before_f > 0, before_f, leak_slope * before_f).astype(jnp.bfloat16)
    turned = grad_out[0].reshape(parts, half_x * plane, rows).transpose(0, 2, 1)
    following = jnp.pad(turned[1:, :, :plane], ((0, 1), (0, 0), (0, 0)))
    pieces = jnp.concatenate([turned, following], axis=2)
    shard = weight_two.reshape(rows, 27, channels).transpose(1, 0, 2)
    shard = jnp.pad(shard, ((0, 1), (0, 0), (0, 0))).reshape(28 * rows, channels)
    weights, grads = gathered(groups, parts, shard, pieces)
    weights = weights.reshape(parts, 28, rows, channels).transpose(1, 0, 2, 3)
    weights = weights.reshape(28, filters, channels)
    grads = grads.reshape(filters, (half_x + 1) * plane)
    upper = grads.T.reshape(half_x + 1, half_y, half_z, filters)
    below = passed_along(hidden[-1:], "space", 1)
    upper = jnp.pad(upper, ((0, 0), (0, 1), (0, 1), (0, 0)))
    back = transpose_conv(upper, weights)
    delta = (back * jnp.where(before_f > 0, 1.0, leak_slope)).astype(jnp.bfloat16)
    framed = padded_2(acts, (("space", 0),), 1)
    framed = jnp.pad(framed, ((0, 0), (1, 1), (1, 1), (0, 0)))
    terms = coarse_terms(hidden, below, grads[:, : half_x * plane], (half_x, half_y, half_z))
    terms = terms + fine_terms(framed, delta)
    totals = reduced(groups, parts, scaling, terms)
    totals = totals.reshape(-1, rows, channels)
    shape = (rows, 3, 3, 3, channels)
    coarse = totals[:27].transpose(1, 0, 2).reshape(shape)
    fine = totals[27:54].transpose(1, 0, 2).reshape(shape)
    return (fine, coarse)


def solution(mesh):
    placed = (
        P("dp", "space", None, None, None),
        P("dp", "space", None, None, None),
        P("space", None, None, None, None),
        P("dp", None, None, None, "space"),
    )
    return jax.shard_map(
        body,
        mesh=mesh,
        in_specs=placed,
        out_specs=(P("space", None, None, None, None), P("space", None, None, None, None)),
        check_vma=False,
    )
```

```python
import functools
import math

import jax
import jax.numpy as jnp
from jax import lax
from jax.experimental import pallas as pl
from jax.experimental.pallas import tpu as pltpu
from jax.sharding import PartitionSpec as P

leak_slope = 0.3
parity_taps = {0: ((1, 0),), 1: ((0, 1), (2, 0))}
MESH = pl.DeviceIdType.MESH
VMEM = pltpu.VMEM
f32, bf16 = jnp.float32, jnp.bfloat16


def remote(src, dst, send, recv, target):
    return pltpu.make_async_remote_copy(
        src_ref=src,
        dst_ref=dst,
        send_sem=send,
        recv_sem=recv,
        device_id=target,
        device_id_type=MESH,
    )


def greet(dp, parts):
    me, mine = lax.axis_index("space"), lax.axis_index("dp")
    barrier = pltpu.get_barrier_semaphore()
    for d in range(1, parts):
        pl.semaphore_signal(
            barrier, inc=1, device_id={"space": lax.rem(me + d, parts)}, device_id_type=MESH
        )
    for d in range(1, dp):
        pl.semaphore_signal(
            barrier, inc=1, device_id={"dp": lax.rem(mine + d, dp)}, device_id_type=MESH
        )
    pl.semaphore_wait(barrier, parts + dp - 2)


class Reduction:
    def __init__(self, dp, parts, scaling, out, part, scratch):
        self.dp, self.parts, self.scaling, self.out, self.part = dp, parts, scaling, out, part
        self.got, self.away, self.came, self.apart, self.near, self.whole, self.sends, self.recvs = scratch
        self.me, self.mine = lax.axis_index("space"), lax.axis_index("dp")
        self.core = lax.rem(self.mine, 2)
        self.rest = self.mine // 2
        self.ranks = dp // 2
        self.chunk = part.shape[0] // dp
        self.half = self.chunk * self.ranks
        self.order = list(range(1, self.ranks)) + [0]
        self.rows = part.shape[1] // parts
        self.inputs = part.shape[2]

    def to_core(self):
        self.first = []
        theirs = (1 - self.core) * self.half
        for d in self.order:
            j = lax.rem(self.rest + d, self.ranks)
            copy = remote(
                self.part.at[pl.ds(theirs + j * self.chunk, self.chunk)],
                self.got.at[d],
                self.sends.at[0, d],
                self.recvs.at[0, d],
                {"dp": self.mine + 1 - 2 * self.core},
            )
            copy.start()
            self.first.append(copy)

    def to_chips(self):
        self.second = []
        for d, copy in zip(self.order, self.first):
            j = lax.rem(self.rest + d, self.ranks)
            base = self.core * self.half + j * self.chunk
            copy.wait_recv()
            if d:

                def fill(u, carry):
                    self.away[d - 1, u] = (self.part[base + u] + self.got[d, u]).astype(bf16)
                    return carry

                lax.fori_loop(0, self.chunk, fill, 0)
                onward = remote(
                    self.away.at[d - 1],
                    self.came.at[d - 1],
                    self.sends.at[1, d],
                    self.recvs.at[1, d],
                    {"dp": 2 * j + self.core},
                )
                onward.start()
                self.second.append(onward)

    def to_space(self):
        base = self.core * self.half + self.rest * self.chunk
        for onward in self.second:
            onward.wait_recv()

        def settle(u, carry):
            total = self.part[base + u] + self.got[0, u]
            for d in range(1, self.ranks):
                total = total + self.came[d - 1, u].astype(f32)
            self.got[0, u] = total
            return carry

        lax.fori_loop(0, self.chunk, settle, 0)
        self.third = []
        for d in range(1, self.parts):
            t = lax.rem(self.me + d, self.parts)
            self.apart[d - 1] = self.block(t).astype(bf16)
            copy = remote(
                self.apart.at[d - 1],
                self.near.at[d - 1],
                self.sends.at[2, d],
                self.recvs.at[2, d],
                {"space": t},
            )
            copy.start()
            self.third.append(copy)

    def block(self, t):
        start = pl.multiple_of(t * self.rows, self.rows)
        taps = self.got[0, :, pl.ds(start, self.rows), :]
        return taps.reshape(self.chunk * self.rows, self.inputs)

    def to_copies(self):
        total = self.block(self.me)
        for d in range(1, self.parts):
            self.third[d - 1].wait_recv()
            total = total + self.near[d - 1].astype(f32)
        self.whole[0] = total * self.scaling
        self.fourth = []
        for d in range(1, self.dp):
            copy = remote(
                self.whole.at[0],
                self.whole.at[d],
                self.sends.at[3, d],
                self.recvs.at[3, d],
                {"dp": lax.rem(self.mine + d, self.dp)},
            )
            copy.start()
            self.fourth.append(copy)

    def finish(self):
        self.out[self.core * self.ranks + self.rest] = self.whole[0]
        for d in range(1, self.dp):
            self.fourth[d - 1].wait_recv()
            other = lax.rem(self.mine + self.dp - d, self.dp)
            self.out[lax.rem(other, 2) * self.ranks + other // 2] = self.whole[d]
        for copy in self.first + self.second + self.third + self.fourth:
            copy.wait_send()


def kernel(dp, parts, scaling, sizes, acts, pre, w_ref, g_ref, coarse_out, fine_out, *scratch):
    coarse_sum = Reduction(dp, parts, scaling, coarse_out, scratch[0], scratch[1:9])
    fine_sum = Reduction(dp, parts, scaling, fine_out, scratch[9], scratch[10:18])
    (wbuf, gbuf, halo, sends, recvs, w_full, mixing, g_turned, g_rows, values, thin, frame, delta) = scratch[18:]
    coarse, fine = scratch[0], scratch[9]
    depth, across, height, channels = sizes
    half_x, half_y, half_z = depth // 2, across // 2, height // 2
    plane, small = across * height, half_y * half_z
    rows = channels // parts
    me, mine = lax.axis_index("space"), lax.axis_index("dp")
    core = lax.rem(mine, 2)
    partner = mine + 1 - 2 * core
    half = w_ref.shape[0] // 2
    greet(dp, parts)

    g_copies, w_copies, forwards = [], [], []
    for d in range(1, parts):
        t = lax.rem(me + d, parts)
        copy = remote(g_ref.at[t], gbuf.at[d - 1], sends.at[0, d], recvs.at[0, d], {"space": t})
        copy.start()
        g_copies.append(copy)
    own = w_ref.at[pl.ds(pl.multiple_of(core * half, 16), half)]
    for d in range(1, parts):
        t = lax.rem(me + d, parts)
        copy = remote(own, wbuf.at[d - 1, core], sends.at[1, d], recvs.at[1, d], {"space": t})
        copy.start()
        w_copies.append(copy)
    upward = remote(
        acts.at[depth - 1],
        halo.at[0],
        sends.at[2, 0],
        recvs.at[2, 0],
        {"space": lax.rem(me + 1, parts)},
    )
    downward = remote(
        acts.at[0],
        halo.at[1],
        sends.at[0, 0],
        recvs.at[0, 0],
        {"space": lax.rem(me + parts - 1, parts)},
    )
    pl.when(me < parts - 1)(upward.start)
    pl.when(me > 0)(downward.start)

    at_z = lax.broadcasted_iota(jnp.int32, (small, channels), 0) % half_z

    def spread(x, carry):
        values[x] = pre[x].astype(f32).reshape(half_y, 2, height, channels)
        for odd_y in (0, 1):
            pair = []
            for odd_z in (0, 1):
                cells = values[x, :, odd_y, pl.ds(odd_z, half_z, stride=2), :]
                cells = cells.reshape(small, channels)
                pair.append(jnp.where(cells > 0, cells, leak_slope * cells))
            earlier = jnp.where(at_z == 0, 0.0, pltpu.roll(pair[1], 1, 0))
            row = half_z * odd_y
            thin[x, odd_y, pl.ds(row, small), 0:channels] = earlier.astype(bf16)
            thin[x, odd_y, pl.ds(row, small), channels : 2 * channels] = pair[0].astype(bf16)
            thin[x, odd_y, pl.ds(row, small), 2 * channels :] = pair[1].astype(bf16)
        thin[x, 1, 0:half_z, :] = jnp.zeros((half_z, 3 * channels), bf16)
        return carry

    lax.fori_loop(0, depth, spread, 0)

    at_cell = lax.broadcasted_iota(jnp.int32, (plane, channels), 0) % height

    def place(q, cells):
        cells = cells.astype(f32)
        inner = pl.ds(height, plane)
        earlier = jnp.where(at_cell == 0, 0.0, pltpu.roll(cells, 1, 0))
        later = jnp.where(at_cell == height - 1, 0.0, pltpu.roll(cells, plane - 1, 0))
        frame[q, inner, 0:channels] = earlier.astype(bf16)
        frame[q, inner, channels : 2 * channels] = cells.astype(bf16)
        frame[q, inner, 2 * channels :] = later.astype(bf16)
        nothing = jnp.zeros((height, 3 * channels), bf16)
        frame[q, 0:height, :] = nothing
        frame[q, pl.ds(height + plane, height), :] = nothing

    def place_own(x, carry):
        place(x + 1, acts[x])
        return carry

    lax.fori_loop(0, depth, place_own, 0)

    def take_filters(s, part, block):
        block = block.astype(f32).reshape(half // rows, rows, channels)
        start = pl.multiple_of(s * rows, rows)
        w_full[pl.ds(part * (half // rows), half // rows), pl.ds(start, rows), :] = block

    def take_cotangents(s, block):
        g_turned[pl.ds(pl.multiple_of(s * rows, rows), rows), :] = block.astype(f32)

    take_cotangents(me, g_ref[me])
    for part in (0, 1):
        take_filters(me, part, w_ref[part * half : (part + 1) * half])
    for d in range(1, parts):
        g_copies[d - 1].wait_recv()
        take_cotangents(lax.rem(me + parts - d, parts), gbuf[d - 1])
    for d in range(1, parts):
        w_copies[d - 1].wait_recv()
        block = wbuf.at[d - 1, core]
        copy = remote(block, block, sends.at[2, d], recvs.at[2, d], {"dp": partner})
        copy.start()
        forwards.append(copy)

    for tap_x in range(3):
        for tap_y in range(3):
            total = None
            for p in range(half_x):
                at_p, at_x = (p + 1, 2 * p + 1) if tap_x == 0 else (p, 2 * p + tap_x - 1)
                lhs = g_turned[:, at_p * small : (at_p + 1) * small].astype(bf16)
                row = half_z if tap_y == 2 else 0
                rhs = thin[at_x, 0 if tap_y == 1 else 1, row : row + small, :]
                term = jnp.dot(lhs, rhs, preferred_element_type=f32)
                total = term if total is None else total + term
            for tap_z in range(3):
                coarse[9 * tap_x + 3 * tap_y + tap_z] = total[
                    :, tap_z * channels : (tap_z + 1) * channels
                ]
    for u in range(27, coarse.shape[0]):
        coarse[u] = jnp.zeros((channels, channels), f32)
    coarse_sum.to_core()

    for p in range(half_x + 1):
        cells = g_turned[:, p * small : (p + 1) * small].T
        later = jnp.where(at_z == half_z - 1, 0.0, pltpu.roll(cells, small - 1, 0))
        g_rows[p, 0:small, 0:channels] = cells.astype(bf16)
        g_rows[p, 0:small, channels:] = later.astype(bf16)
        g_rows[p, small : small + half_z, :] = jnp.zeros((half_z, 2 * channels), bf16)

    for d in range(1, parts):
        forwards[d - 1].wait_recv()
        s = lax.rem(me + parts - d, parts)
        for part in (0, 1):
            take_filters(s, part, wbuf[d - 1, part])

    def mix(t, carry):
        mixing[t, 0:channels, 0:channels] = w_full[3 * t + 1].astype(bf16)
        mixing[t, 0:channels, channels:] = w_full[3 * t + 2].astype(bf16)
        mixing[t, channels:, 0:channels] = jnp.zeros((channels, channels), bf16)
        mixing[t, channels:, channels:] = w_full[3 * t].astype(bf16)
        return carry

    lax.fori_loop(0, 9, mix, 0)
    coarse_sum.to_chips()

    def propagate(p, carry):
        for odd_x in (0, 1):
            for odd_y in (0, 1):
                total = None
                for tap_x, move_x in parity_taps[odd_x]:
                    for tap_y, move_y in parity_taps[odd_y]:
                        cells = g_rows[p + move_x, move_y * half_z : move_y * half_z + small, :]
                        term = jnp.dot(
                            cells, mixing[3 * tap_x + tap_y], preferred_element_type=f32
                        )
                        total = term if total is None else total + term
                for odd_z in (0, 1):
                    where = (2 * p + odd_x, slice(None), odd_y, pl.ds(odd_z, half_z, stride=2))
                    before = values[where].reshape(small, channels)
                    piece = total[:, odd_z * channels : (odd_z + 1) * channels]
                    piece = piece * jnp.where(before > 0, 1.0, leak_slope)
                    values[where] = piece.reshape(half_y, half_z, channels)
        for odd_x in (0, 1):
            x = 2 * p + odd_x
            cells = values[x].reshape(plane, channels)
            delta[pl.ds(pl.multiple_of(x * channels, channels), channels), :] = cells.T.astype(bf16)
        return carry

    lax.fori_loop(0, half_x, propagate, 0)

    def clear(u, carry):
        fine[u] = jnp.zeros((channels, channels), f32)
        return carry

    lax.fori_loop(0, fine.shape[0], clear, 0)

    def layer(q):
        low, high = max(0, q - 2), min(depth - 1, q)

        def step(tap_y, carry):
            rhs = frame[q, pl.ds(pl.multiple_of(tap_y * height, height), plane), :]
            lhs = delta[low * channels : (high + 1) * channels, :]
            total = jnp.dot(lhs, rhs, preferred_element_type=f32)
            for x in range(low, high + 1):
                for tap_z in range(3):
                    fine[9 * (q - x) + 3 * tap_y + tap_z] += total[
                        (x - low) * channels : (x - low + 1) * channels,
                        tap_z * channels : (tap_z + 1) * channels,
                    ]
            return carry

        lax.fori_loop(0, 3, step, 0)

    layer(1)
    coarse_sum.to_space()
    for q in range(2, depth):
        layer(q)
    coarse_sum.to_copies()
    layer(depth)

    @pl.when(me > 0)
    def _():
        upward.wait_recv()
        place(0, halo[0])
        layer(0)

    @pl.when(me < parts - 1)
    def _():
        downward.wait_recv()
        place(depth + 1, halo[1])
        layer(depth + 1)

    fine_sum.to_core()
    coarse_sum.finish()
    fine_sum.to_chips()
    fine_sum.to_space()
    fine_sum.to_copies()
    fine_sum.finish()
    for copy in g_copies + w_copies + forwards:
        copy.wait_send()
    pl.when(me < parts - 1)(upward.wait_send)
    pl.when(me > 0)(downward.wait_send)


def reduction_scratch(dp, parts, channels):
    chunk = -(-27 // dp)
    ranks = dp // 2
    rows = channels // parts
    most = max(dp, parts)
    return [
        VMEM((chunk * dp, channels, channels), f32),
        VMEM((ranks, chunk, channels, channels), f32),
        VMEM((ranks - 1, chunk, channels, channels), bf16),
        VMEM((ranks - 1, chunk, channels, channels), bf16),
        VMEM((parts - 1, chunk * rows, channels), bf16),
        VMEM((parts - 1, chunk * rows, channels), bf16),
        VMEM((dp, chunk * rows, channels), f32),
        pltpu.SemaphoreType.DMA((4, most)),
        pltpu.SemaphoreType.DMA((4, most)),
    ]


def gradients(dp, parts, scaling, sizes, acts, pre, w, g):
    depth, across, height, channels = sizes
    half_x, half_y, half_z = depth // 2, across // 2, height // 2
    plane, small = across * height, half_y * half_z
    chunk = -(-27 // dp)
    rows = channels // parts
    half = w.shape[0] // 2
    flops = 2 * 27 * channels * channels * (depth * plane + 2 * half_x * small)
    return pl.pallas_call(
        functools.partial(kernel, dp, parts, scaling, sizes),
        out_shape=[jax.ShapeDtypeStruct((dp, chunk * rows, channels), f32)] * 2,
        in_specs=[pl.BlockSpec(memory_space=VMEM)] * 4,
        out_specs=[pl.BlockSpec(memory_space=VMEM)] * 2,
        scratch_shapes=reduction_scratch(dp, parts, channels)
        + reduction_scratch(dp, parts, channels)
        + [
            VMEM((parts - 1, 2, half, channels), bf16),
            VMEM((parts - 1,) + g.shape[1:], bf16),
            VMEM((2, plane, channels), bf16),
            pltpu.SemaphoreType.DMA((3, parts)),
            pltpu.SemaphoreType.DMA((3, parts)),
            VMEM((28, channels, channels), f32),
            VMEM((9, 2 * channels, 2 * channels), bf16),
            VMEM((channels, (half_x + 1) * small), f32),
            VMEM((half_x + 1, small + half_z, 2 * channels), bf16),
            VMEM((depth, half_y, 2, height, channels), f32),
            VMEM((depth, 2, small + half_z, 3 * channels), bf16),
            VMEM((depth + 2, plane + 2 * height, 3 * channels), bf16),
            VMEM((depth * channels, plane), bf16),
        ],
        cost_estimate=pl.CostEstimate(flops=flops, bytes_accessed=8 << 20, transcendentals=0),
        compiler_params=pltpu.CompilerParams(
            collective_id=0, has_side_effects=True, vmem_limit_bytes=56 << 20
        ),
    )(acts, pre, w, g)


def body(acts_in, pre_act, weight_two, grad_out):
    parts = lax.axis_size("space")
    groups = lax.axis_size("dp")
    depth, across, height, channels = sizes = acts_in.shape[1:]
    rows = weight_two.shape[0]
    scaling = 1.0 / math.sqrt(groups * depth * parts * across * height)
    small = across * height // 4
    turned = grad_out[0].reshape(parts, depth // 2 * small, rows).transpose(0, 2, 1)
    following = jnp.pad(turned[1:, :, :small], ((0, 1), (0, 0), (0, 0)))
    pieces = jnp.concatenate([turned, following], axis=2)
    shard = weight_two.reshape(rows, 27, channels).transpose(1, 0, 2)
    shard = jnp.pad(shard, ((0, 1), (0, 0), (0, 0))).reshape(28 * rows, channels)
    flat = (depth, across * height, channels)
    coarse, fine = gradients(
        groups, parts, scaling, sizes, acts_in.reshape(flat), pre_act.reshape(flat), shard, pieces
    )

    def by_filter(totals):
        taps = totals.reshape(-1, rows, channels)[:27]
        return taps.transpose(1, 0, 2).reshape(rows, 3, 3, 3, channels)

    return (by_filter(fine), by_filter(coarse))


def solution(mesh):
    placed = (
        P("dp", "space", None, None, None),
        P("dp", "space", None, None, None),
        P("space", None, None, None, None),
        P("dp", None, None, None, "space"),
    )
    return jax.shard_map(
        body,
        mesh=mesh,
        in_specs=placed,
        out_specs=(P("space", None, None, None, None), P("space", None, None, None, None)),
        check_vma=False,
    )
```

```python
import functools
import math

import jax
import jax.numpy as jnp
from jax import lax
from jax.experimental import pallas as pl
from jax.experimental.pallas import tpu as pltpu
from jax.sharding import PartitionSpec as P

leak_slope = 0.3
parity_taps = {0: ((1, 0),), 1: ((0, 1), (2, 0))}
MESH = pl.DeviceIdType.MESH
VMEM = pltpu.VMEM
f32, bf16 = jnp.float32, jnp.bfloat16


def remote(src, dst, send, recv, target):
    return pltpu.make_async_remote_copy(
        src_ref=src,
        dst_ref=dst,
        send_sem=send,
        recv_sem=recv,
        device_id=target,
        device_id_type=MESH,
    )


def hello(dp, parts):
    me, mine = lax.axis_index("space"), lax.axis_index("dp")
    barrier = pltpu.get_barrier_semaphore()
    for d in range(1, parts):
        pl.semaphore_signal(
            barrier, inc=1, device_id={"space": lax.rem(me + d, parts)}, device_id_type=MESH
        )
    for d in range(1, dp):
        pl.semaphore_signal(
            barrier, inc=1, device_id={"dp": lax.rem(mine + d, dp)}, device_id_type=MESH
        )


class Reduction:
    def __init__(self, dp, parts, scaling, out, place, part, scratch):
        self.place = place
        self.dp, self.parts, self.scaling, self.out, self.part = dp, parts, scaling, out, part
        self.got, self.away, self.came, self.apart, self.near, self.whole, self.sends, self.recvs = scratch
        self.me, self.mine = lax.axis_index("space"), lax.axis_index("dp")
        self.core = lax.rem(self.mine, 2)
        self.rest = self.mine // 2
        self.ranks = dp // 2
        self.chunk = part.shape[0] // dp
        self.half = self.chunk * self.ranks
        self.order = list(range(1, self.ranks)) + [0]
        self.rows = part.shape[1] // parts
        self.inputs = part.shape[2]

    def to_core(self):
        self.first = []
        theirs = (1 - self.core) * self.half
        for d in self.order:
            j = lax.rem(self.rest + d, self.ranks)
            copy = remote(
                self.part.at[pl.ds(theirs + j * self.chunk, self.chunk)],
                self.got.at[d],
                self.sends.at[0, d],
                self.recvs.at[0, d],
                {"dp": self.mine + 1 - 2 * self.core},
            )
            copy.start()
            self.first.append(copy)

    def to_chips(self):
        self.second = []
        for d, copy in zip(self.order, self.first):
            j = lax.rem(self.rest + d, self.ranks)
            base = self.core * self.half + j * self.chunk
            copy.wait_recv()
            if d:

                def fill(u, carry):
                    self.away[d - 1, u] = (self.part[base + u] + self.got[d, u]).astype(bf16)
                    return carry

                lax.fori_loop(0, self.chunk, fill, 0)
                onward = remote(
                    self.away.at[d - 1],
                    self.came.at[d - 1],
                    self.sends.at[1, d],
                    self.recvs.at[1, d],
                    {"dp": 2 * j + self.core},
                )
                onward.start()
                self.second.append(onward)

    def to_space(self):
        base = self.core * self.half + self.rest * self.chunk
        for onward in self.second:
            onward.wait_recv()

        def settle(u, carry):
            total = self.part[base + u] + self.got[0, u]
            for d in range(1, self.ranks):
                total = total + self.came[d - 1, u].astype(f32)
            self.got[0, u] = total
            return carry

        lax.fori_loop(0, self.chunk, settle, 0)
        self.third = []
        for d in range(1, self.parts):
            t = lax.rem(self.me + d, self.parts)
            self.apart[d - 1] = self.block(t).astype(bf16)
            copy = remote(
                self.apart.at[d - 1],
                self.near.at[d - 1],
                self.sends.at[2, d],
                self.recvs.at[2, d],
                {"space": t},
            )
            copy.start()
            self.third.append(copy)

    def block(self, t):
        start = pl.multiple_of(t * self.rows, self.rows)
        taps = self.got[0, :, pl.ds(start, self.rows), :]
        return taps.reshape(self.chunk * self.rows, self.inputs)

    def to_copies(self):
        total = self.block(self.me)
        for d in range(1, self.parts):
            self.third[d - 1].wait_recv()
            total = total + self.near[d - 1].astype(f32)
        self.whole[0] = total * self.scaling
        self.fourth = []
        for d in range(1, self.dp):
            copy = remote(
                self.whole.at[0],
                self.whole.at[d],
                self.sends.at[3, d],
                self.recvs.at[3, d],
                {"dp": lax.rem(self.mine + d, self.dp)},
            )
            copy.start()
            self.fourth.append(copy)

    def put(self, c, d):
        for u in range(self.chunk):
            taps = self.whole[d, u * self.rows : (u + 1) * self.rows, :]
            self.out[self.place(c * self.chunk + u)] = taps

    def finish(self):
        self.put(self.core * self.ranks + self.rest, 0)
        for d in range(1, self.dp):
            self.fourth[d - 1].wait_recv()
            other = lax.rem(self.mine + self.dp - d, self.dp)
            self.put(lax.rem(other, 2) * self.ranks + other // 2, d)
        for copy in self.first + self.second + self.third + self.fourth:
            copy.wait_send()


def middle_place(u):
    return u + 9 + 18 * (u // 9)


def outer_place(u):
    return u + 9 * (u // 9)


def kernel(dp, parts, scaling, sizes, acts, pre, w_ref, g_ref, coarse_out, fine_out, *scratch):
    coarse, middle, outer = scratch[0], scratch[9], scratch[18]
    share = (dp, parts, scaling)
    coarse_sum = Reduction(*share, coarse_out, lambda u: u, coarse, scratch[1:9])
    middle_sum = Reduction(*share, fine_out, middle_place, middle, scratch[10:18])
    outer_sum = Reduction(*share, fine_out, outer_place, outer, scratch[19:27])
    (wbuf, gbuf, halo, sends, recvs, w_full, mixing, g_send, g_turned, g_mixed, g_cells, g_rows, values, thin, frame, delta) = scratch[27:]
    depth, across, height, channels = sizes
    half_x, half_y, half_z = depth // 2, across // 2, height // 2
    plane, small = across * height, half_y * half_z
    rows = channels // parts
    me, mine = lax.axis_index("space"), lax.axis_index("dp")
    core = lax.rem(mine, 2)
    partner = mine + 1 - 2 * core
    half = (w_ref.shape[0] + 1) // 2
    beside = me + 1 - 2 * lax.rem(me, 2)
    hello(dp, parts)

    count = 128 // half_y

    def pack(x, carry):
        for group in range(half_z // count):
            cells = [g_ref[x, group * count + j].astype(f32) for j in range(count)]
            g_send[x, :, group * 128 : (group + 1) * 128] = jnp.concatenate(cells, axis=1).astype(bf16)
        return carry

    lax.fori_loop(0, g_ref.shape[0], pack, 0)
    g_send[g_ref.shape[0]] = jnp.zeros((rows, small), bf16)
    pl.semaphore_wait(pltpu.get_barrier_semaphore(), parts + dp - 2)

    g_copies, w_copies, w_beside, forwards = [], [], [], []
    for d in range(1, parts):
        t = lax.rem(me + d, parts)
        mine_there = g_send.at[pl.ds(t * half_x, half_x + 1)]
        copy = remote(mine_there, gbuf.at[d - 1], sends.at[0, d], recvs.at[0, d], {"space": t})
        copy.start()
        g_copies.append(copy)
    own = w_ref.at[pl.ds(core * (half - 1), half)]
    for i in range(1, parts // 2):
        t = lax.rem(me + 2 * i, parts)
        copy = remote(own, wbuf.at[0, i, core], sends.at[1, i], recvs.at[1, i], {"space": t})
        copy.start()
        w_copies.append(copy)
    copy = remote(own, wbuf.at[1, 0, core], sends.at[2, 0], recvs.at[2, 0], {"space": beside})
    copy.start()
    w_beside.append(copy)
    upward = remote(
        acts.at[depth - 1],
        halo.at[0],
        sends.at[5, 0],
        recvs.at[5, 0],
        {"space": lax.rem(me + 1, parts)},
    )
    downward = remote(
        acts.at[0],
        halo.at[1],
        sends.at[5, 1],
        recvs.at[5, 1],
        {"space": lax.rem(me + parts - 1, parts)},
    )

    at_z = lax.broadcasted_iota(jnp.int32, (small, channels), 0) % half_z

    def spread(x, carry):
        values[x] = pre[x].astype(f32).reshape(half_y, 2, height, channels)
        for odd_y in (0, 1):
            pair = []
            for odd_z in (0, 1):
                cells = values[x, :, odd_y, pl.ds(odd_z, half_z, stride=2), :]
                cells = cells.reshape(small, channels)
                pair.append(jnp.where(cells > 0, cells, leak_slope * cells))
            earlier = jnp.where(at_z == 0, 0.0, pltpu.roll(pair[1], 1, 0))
            row = half_z * odd_y
            thin[x, odd_y, pl.ds(row, small), 0:channels] = earlier.astype(bf16)
            thin[x, odd_y, pl.ds(row, small), channels : 2 * channels] = pair[0].astype(bf16)
            thin[x, odd_y, pl.ds(row, small), 2 * channels :] = pair[1].astype(bf16)
        thin[x, 1, 0:half_z, :] = jnp.zeros((half_z, 3 * channels), bf16)
        return carry

    lax.fori_loop(0, depth, spread, 0)

    at_cell = lax.broadcasted_iota(jnp.int32, (plane, channels), 0) % height

    def place(q, cells):
        cells = cells.astype(f32)
        inner = pl.ds(height, plane)
        earlier = jnp.where(at_cell == 0, 0.0, pltpu.roll(cells, 1, 0))
        later = jnp.where(at_cell == height - 1, 0.0, pltpu.roll(cells, plane - 1, 0))
        frame[q, inner, 0:channels] = earlier.astype(bf16)
        frame[q, inner, channels : 2 * channels] = cells.astype(bf16)
        frame[q, inner, 2 * channels :] = later.astype(bf16)
        nothing = jnp.zeros((height, 3 * channels), bf16)
        frame[q, 0:height, :] = nothing
        frame[q, pl.ds(height + plane, height), :] = nothing

    def place_own(x, carry):
        place(x + 1, acts[x])
        return carry

    lax.fori_loop(0, depth, place_own, 0)

    def take_cotangents(s, block):
        start = pl.multiple_of(s * rows, rows)
        g_turned[:, pl.ds(start, rows), :] = block.astype(f32)

    take_cotangents(me, g_send[pl.ds(me * half_x, half_x + 1)])
    for d in range(1, parts):
        g_copies[d - 1].wait_recv()
        take_cotangents(lax.rem(me + parts - d, parts), gbuf[d - 1])
    for p in range(half_x + 1):
        g_mixed[p] = g_turned[p].T
        for y in range(half_y):
            cells = g_mixed[p, pl.ds(y, half_z, stride=half_y), :]
            g_cells[p, y * half_z : (y + 1) * half_z, :] = cells
        g_turned[p] = g_cells[p].T

    for i in range(1, parts // 2):
        w_copies[i - 1].wait_recv()
        block = wbuf.at[0, i, core]
        copy = remote(block, wbuf.at[1, i, core], sends.at[2, i], recvs.at[2, i], {"space": beside})
        copy.start()
        w_beside.append(copy)
        copy = remote(block, block, sends.at[3, i], recvs.at[3, i], {"dp": partner})
        copy.start()
        forwards.append((0, i, copy))
    pl.when(me < parts - 1)(upward.start)
    pl.when(me > 0)(downward.start)

    for tap_x in range(3):
        for tap_y in range(3):
            total = None
            for p in range(half_x):
                at_p, at_x = (p + 1, 2 * p + 1) if tap_x == 0 else (p, 2 * p + tap_x - 1)
                lhs = g_turned[at_p].astype(bf16)
                row = half_z if tap_y == 2 else 0
                rhs = thin[at_x, 0 if tap_y == 1 else 1, row : row + small, :]
                term = jnp.dot(lhs, rhs, preferred_element_type=f32)
                total = term if total is None else total + term
            for tap_z in range(3):
                coarse[9 * tap_x + 3 * tap_y + tap_z] = total[
                    :, tap_z * channels : (tap_z + 1) * channels
                ]
    for u in range(27, coarse.shape[0]):
        coarse[u] = jnp.zeros((channels, channels), f32)
    coarse_sum.to_core()
    for i in range(parts // 2):
        w_beside[i].wait_recv()
        block = wbuf.at[1, i, core]
        copy = remote(block, block, sends.at[4, i], recvs.at[4, i], {"dp": partner})
        copy.start()
        forwards.append((1, i, copy))

    for p in range(half_x + 1):
        cells = g_cells[p]
        later = jnp.where(at_z == half_z - 1, 0.0, pltpu.roll(cells, small - 1, 0))
        g_rows[p, 0:small, 0:channels] = cells.astype(bf16)
        g_rows[p, 0:small, channels:] = later.astype(bf16)
        g_rows[p, small : small + half_z, :] = jnp.zeros((half_z, 2 * channels), bf16)

    def take_filters(s, part, block):
        start = pl.multiple_of(s * rows, rows)
        w_full[pl.ds(part * (half - 1), half), pl.ds(start, rows), :] = block.astype(f32)

    for part in (0, 1):
        take_filters(me, part, w_ref[part * (half - 1) : part * (half - 1) + half])
    for side, i, copy in forwards:
        copy.wait_recv()
        source = beside if side else me
        for part in (0, 1):
            take_filters(lax.rem(source + parts - 2 * i, parts), part, wbuf[side, i, part])

    def mix(t, carry):
        mixing[t, 0:channels, 0:channels] = w_full[3 * t + 1].astype(bf16)
        mixing[t, 0:channels, channels:] = w_full[3 * t + 2].astype(bf16)
        mixing[t, channels:, 0:channels] = jnp.zeros((channels, channels), bf16)
        mixing[t, channels:, channels:] = w_full[3 * t].astype(bf16)
        return carry

    lax.fori_loop(0, 9, mix, 0)
    coarse_sum.to_chips()

    def propagate(p, carry):
        for odd_x in (0, 1):
            for odd_y in (0, 1):
                total = None
                for tap_x, move_x in parity_taps[odd_x]:
                    for tap_y, move_y in parity_taps[odd_y]:
                        cells = g_rows[p + move_x, move_y * half_z : move_y * half_z + small, :]
                        term = jnp.dot(
                            cells, mixing[3 * tap_x + tap_y], preferred_element_type=f32
                        )
                        total = term if total is None else total + term
                for odd_z in (0, 1):
                    where = (2 * p + odd_x, slice(None), odd_y, pl.ds(odd_z, half_z, stride=2))
                    before = values[where].reshape(small, channels)
                    piece = total[:, odd_z * channels : (odd_z + 1) * channels]
                    piece = piece * jnp.where(before > 0, 1.0, leak_slope)
                    values[where] = piece.reshape(half_y, half_z, channels)
        for odd_x in (0, 1):
            x = 2 * p + odd_x
            cells = values[x].reshape(plane, channels)
            delta[pl.ds(pl.multiple_of(x * channels, channels), channels), :] = cells.T.astype(bf16)
        return carry

    lax.fori_loop(0, half_x, propagate, 0)

    def clear(u, carry):
        outer[u] = jnp.zeros((channels, channels), f32)
        return carry

    lax.fori_loop(0, outer.shape[0], clear, 0)
    for u in range(middle.shape[0]):
        middle[u] = jnp.zeros((channels, channels), f32)

    def layer(q):
        low, high = max(0, q - 2), min(depth - 1, q)

        def step(tap_y, carry):
            rhs = frame[q, pl.ds(pl.multiple_of(tap_y * height, height), plane), :]
            lhs = delta[low * channels : (high + 1) * channels, :]
            total = jnp.dot(lhs, rhs, preferred_element_type=f32)
            for x in range(low, high + 1):
                into, first = (middle, 0) if q - x == 1 else (outer, 9 * ((q - x) // 2))
                for tap_z in range(3):
                    into[first + 3 * tap_y + tap_z] += total[
                        (x - low) * channels : (x - low + 1) * channels,
                        tap_z * channels : (tap_z + 1) * channels,
                    ]
            return carry

        lax.fori_loop(0, 3, step, 0)

    layer(1)
    coarse_sum.to_space()
    for q in range(2, depth):
        layer(q)
    coarse_sum.to_copies()
    layer(depth)

    middle_sum.to_core()

    @pl.when(me > 0)
    def _():
        upward.wait_recv()
        place(0, halo[0])
        layer(0)

    middle_sum.to_chips()

    @pl.when(me < parts - 1)
    def _():
        downward.wait_recv()
        place(depth + 1, halo[1])
        layer(depth + 1)

    outer_sum.to_core()
    middle_sum.to_space()
    outer_sum.to_chips()
    coarse_sum.finish()
    middle_sum.to_copies()
    outer_sum.to_space()
    middle_sum.finish()
    outer_sum.to_copies()
    outer_sum.finish()
    for copy in g_copies + w_copies + w_beside + [copy for _, _, copy in forwards]:
        copy.wait_send()
    pl.when(me < parts - 1)(upward.wait_send)
    pl.when(me > 0)(downward.wait_send)


def reduction_scratch(dp, parts, channels, taps):
    chunk = -(-taps // dp)
    ranks = dp // 2
    rows = channels // parts
    most = max(dp, parts)
    return [
        VMEM((chunk * dp, channels, channels), f32),
        VMEM((ranks, chunk, channels, channels), f32),
        VMEM((ranks - 1, chunk, channels, channels), bf16),
        VMEM((ranks - 1, chunk, channels, channels), bf16),
        VMEM((parts - 1, chunk * rows, channels), bf16),
        VMEM((parts - 1, chunk * rows, channels), bf16),
        VMEM((dp, chunk * rows, channels), f32),
        pltpu.SemaphoreType.DMA((4, most)),
        pltpu.SemaphoreType.DMA((4, most)),
    ]


def gradients(dp, parts, scaling, sizes, acts, pre, w, g):
    depth, across, height, channels = sizes
    half_x, half_y, half_z = depth // 2, across // 2, height // 2
    plane, small = across * height, half_y * half_z
    chunk = -(-27 // dp)
    rows = channels // parts
    half = (w.shape[0] + 1) // 2
    units = [chunk * dp]
    for taps, where in ((9, middle_place), (18, outer_place)):
        units.append(where(-(-taps // dp) * dp - 1) + 1)
    flops = 2 * 27 * channels * channels * (depth * plane + 2 * half_x * small)
    return pl.pallas_call(
        functools.partial(kernel, dp, parts, scaling, sizes),
        out_shape=[
            jax.ShapeDtypeStruct((n, rows, channels), f32) for n in (units[0], max(units[1:]))
        ],
        in_specs=[pl.BlockSpec(memory_space=VMEM)] * 4,
        out_specs=[pl.BlockSpec(memory_space=VMEM)] * 2,
        scratch_shapes=reduction_scratch(dp, parts, channels, 27)
        + reduction_scratch(dp, parts, channels, 9)
        + reduction_scratch(dp, parts, channels, 18)
        + [
            VMEM((2, parts // 2, 2, half, rows, channels), bf16),
            VMEM((parts - 1, half_x + 1, rows, small), bf16),
            VMEM((2, plane, channels), bf16),
            pltpu.SemaphoreType.DMA((6, parts)),
            pltpu.SemaphoreType.DMA((6, parts)),
            VMEM((27, channels, channels), f32),
            VMEM((9, 2 * channels, 2 * channels), bf16),
            VMEM((g.shape[0] + 1, rows, small), bf16),
            VMEM((half_x + 1, channels, small), f32),
            VMEM((half_x + 1, small, channels), f32),
            VMEM((half_x + 1, small, channels), f32),
            VMEM((half_x + 1, small + half_z, 2 * channels), bf16),
            VMEM((depth, half_y, 2, height, channels), f32),
            VMEM((depth, 2, small + half_z, 3 * channels), bf16),
            VMEM((depth + 2, plane + 2 * height, 3 * channels), bf16),
            VMEM((depth * channels, plane), bf16),
        ],
        cost_estimate=pl.CostEstimate(flops=flops, bytes_accessed=8 << 20, transcendentals=0),
        compiler_params=pltpu.CompilerParams(
            collective_id=0, has_side_effects=True, vmem_limit_bytes=56 << 20
        ),
    )(acts, pre, w, g)


def body(acts_in, pre_act, weight_two, grad_out):
    parts = lax.axis_size("space")
    groups = lax.axis_size("dp")
    depth, across, height, channels = sizes = acts_in.shape[1:]
    rows = weight_two.shape[0]
    scaling = 1.0 / math.sqrt(groups * depth * parts * across * height)
    turned = grad_out[0].transpose(0, 2, 3, 1)
    shard = weight_two.reshape(rows, 27, channels).transpose(1, 0, 2)
    flat = (depth, across * height, channels)
    coarse, fine = gradients(
        groups, parts, scaling, sizes, acts_in.reshape(flat), pre_act.reshape(flat), shard, turned
    )

    def by_filter(totals):
        taps = totals[:27]
        return taps.transpose(1, 0, 2).reshape(rows, 3, 3, 3, channels)

    return (by_filter(fine), by_filter(coarse))


def solution(mesh):
    placed = (
        P("dp", "space", None, None, None),
        P("dp", "space", None, None, None),
        P("space", None, None, None, None),
        P("dp", None, None, None, "space"),
    )
    return jax.shard_map(
        body,
        mesh=mesh,
        in_specs=placed,
        out_specs=(P("space", None, None, None, None), P("space", None, None, None, None)),
        check_vma=False,
    )
```

```python
import functools
import math

import jax
import jax.numpy as jnp
from jax import lax
from jax.experimental import pallas as pl
from jax.experimental.pallas import tpu as pltpu
from jax.sharding import PartitionSpec as P

leak_slope = 0.3
parity_taps = {0: ((1, 0),), 1: ((0, 1), (2, 0))}
MESH = pl.DeviceIdType.MESH
VMEM = pltpu.VMEM
f32, bf16 = jnp.float32, jnp.bfloat16


def remote(src, dst, send, recv, target):
    return pltpu.make_async_remote_copy(
        src_ref=src,
        dst_ref=dst,
        send_sem=send,
        recv_sem=recv,
        device_id=target,
        device_id_type=MESH,
    )


def hello(dp, parts):
    me, mine = lax.axis_index("space"), lax.axis_index("dp")
    barrier = pltpu.get_barrier_semaphore()
    for d in range(1, parts):
        pl.semaphore_signal(
            barrier, inc=1, device_id={"space": lax.rem(me + d, parts)}, device_id_type=MESH
        )
    for d in range(1, dp):
        pl.semaphore_signal(
            barrier, inc=1, device_id={"dp": lax.rem(mine + d, dp)}, device_id_type=MESH
        )


class Reduction:
    def __init__(self, dp, parts, scaling, out, place, part, scratch):
        self.place = place
        self.dp, self.parts, self.scaling, self.out, self.part = dp, parts, scaling, out, part
        self.got, self.away, self.came, self.apart, self.near, self.whole, self.sends, self.recvs = scratch
        self.me, self.mine = lax.axis_index("space"), lax.axis_index("dp")
        self.core = lax.rem(self.mine, 2)
        self.rest = self.mine // 2
        self.ranks = dp // 2
        self.chunk = part.shape[0] // dp
        self.half = self.chunk * self.ranks
        self.order = list(range(1, self.ranks)) + [0]
        self.rows = part.shape[1] // parts
        self.inputs = part.shape[2]

    def to_core(self):
        self.first = []
        theirs = (1 - self.core) * self.half
        for d in self.order:
            j = lax.rem(self.rest + d, self.ranks)
            copy = remote(
                self.part.at[pl.ds(theirs + j * self.chunk, self.chunk)],
                self.got.at[d],
                self.sends.at[0, d],
                self.recvs.at[0, d],
                {"dp": self.mine + 1 - 2 * self.core},
            )
            copy.start()
            self.first.append(copy)

    def to_chips(self):
        self.second = []
        for d, copy in zip(self.order, self.first):
            j = lax.rem(self.rest + d, self.ranks)
            base = self.core * self.half + j * self.chunk
            copy.wait_recv()
            if d:

                def fill(u, carry):
                    self.away[d - 1, u] = (self.part[base + u] + self.got[d, u]).astype(bf16)
                    return carry

                lax.fori_loop(0, self.chunk, fill, 0)
                onward = remote(
                    self.away.at[d - 1],
                    self.came.at[d - 1],
                    self.sends.at[1, d],
                    self.recvs.at[1, d],
                    {"dp": 2 * j + self.core},
                )
                onward.start()
                self.second.append(onward)

    def to_space(self):
        base = self.core * self.half + self.rest * self.chunk
        for onward in self.second:
            onward.wait_recv()

        def settle(u, carry):
            total = self.part[base + u] + self.got[0, u]
            for d in range(1, self.ranks):
                total = total + self.came[d - 1, u].astype(f32)
            self.got[0, u] = total
            return carry

        lax.fori_loop(0, self.chunk, settle, 0)
        self.third = []
        for d in range(1, self.parts):
            t = lax.rem(self.me + d, self.parts)
            self.apart[d - 1] = self.block(t).astype(bf16)
            copy = remote(
                self.apart.at[d - 1],
                self.near.at[d - 1],
                self.sends.at[2, d],
                self.recvs.at[2, d],
                {"space": t},
            )
            copy.start()
            self.third.append(copy)

    def block(self, t):
        start = pl.multiple_of(t * self.rows, self.rows)
        taps = self.got[0, :, pl.ds(start, self.rows), :]
        return taps.reshape(self.chunk * self.rows, self.inputs)

    def to_copies(self):
        total = self.block(self.me)
        for d in range(1, self.parts):
            self.third[d - 1].wait_recv()
            total = total + self.near[d - 1].astype(f32)
        self.whole[0] = total * self.scaling
        self.fourth = []
        for d in range(1, self.dp):
            copy = remote(
                self.whole.at[0],
                self.whole.at[d],
                self.sends.at[3, d],
                self.recvs.at[3, d],
                {"dp": lax.rem(self.mine + d, self.dp)},
            )
            copy.start()
            self.fourth.append(copy)

    def put(self, c, d):
        for u in range(self.chunk):
            taps = self.whole[d, u * self.rows : (u + 1) * self.rows, :]
            self.out[self.place(c * self.chunk + u)] = taps

    def finish(self):
        self.put(self.core * self.ranks + self.rest, 0)
        for d in range(1, self.dp):
            self.fourth[d - 1].wait_recv()
            other = lax.rem(self.mine + self.dp - d, self.dp)
            self.put(lax.rem(other, 2) * self.ranks + other // 2, d)
        for copy in self.first + self.second + self.third + self.fourth:
            copy.wait_send()


def middle_place(u):
    return u + 9 + 18 * (u // 9)


def outer_place(u):
    return u + 9 * (u // 9)


def kernel(dp, parts, scaling, sizes, acts_far, pre_far, w_ref, g_ref, coarse_out, fine_out, *scratch):
    coarse, middle, outer = scratch[0], scratch[9], scratch[18]
    share = (dp, parts, scaling)
    coarse_sum = Reduction(*share, coarse_out, lambda u: u, coarse, scratch[1:9])
    middle_sum = Reduction(*share, fine_out, middle_place, middle, scratch[10:18])
    outer_sum = Reduction(*share, fine_out, outer_place, outer, scratch[19:27])
    (wbuf, gbuf, halo, sends, recvs, w_full, mixing, g_send, g_turned, g_mixed, g_cells, g_rows, values, thin, frame, delta, acts, pre, loads) = scratch[27:]
    depth, across, height, channels = sizes
    half_x, half_y, half_z = depth // 2, across // 2, height // 2
    plane, small = across * height, half_y * half_z
    rows = channels // parts
    me, mine = lax.axis_index("space"), lax.axis_index("dp")
    core = lax.rem(mine, 2)
    partner = mine + 1 - 2 * core
    half = (w_ref.shape[0] + 1) // 2
    beside = me + 1 - 2 * lax.rem(me, 2)
    hello(dp, parts)
    load_pre = pltpu.make_async_copy(pre_far, pre, loads.at[0])
    load_acts = pltpu.make_async_copy(acts_far, acts, loads.at[1])
    load_pre.start()
    load_acts.start()

    count = 128 // half_y

    def pack(x, carry):
        for group in range(half_z // count):
            cells = [g_ref[x, group * count + j].astype(f32) for j in range(count)]
            g_send[x, :, group * 128 : (group + 1) * 128] = jnp.concatenate(cells, axis=1).astype(bf16)
        return carry

    lax.fori_loop(0, g_ref.shape[0], pack, 0)
    g_send[g_ref.shape[0]] = jnp.zeros((rows, small), bf16)
    pl.semaphore_wait(pltpu.get_barrier_semaphore(), parts + dp - 2)

    g_copies, w_copies, w_beside, forwards = [], [], [], []
    for d in range(1, parts):
        t = lax.rem(me + d, parts)
        mine_there = g_send.at[pl.ds(t * half_x, half_x + 1)]
        copy = remote(mine_there, gbuf.at[d - 1], sends.at[0, d], recvs.at[0, d], {"space": t})
        copy.start()
        g_copies.append(copy)
    own = w_ref.at[pl.ds(core * (half - 1), half)]
    for i in range(1, parts // 2):
        t = lax.rem(me + 2 * i, parts)
        copy = remote(own, wbuf.at[0, i, core], sends.at[1, i], recvs.at[1, i], {"space": t})
        copy.start()
        w_copies.append(copy)
    copy = remote(own, wbuf.at[1, 0, core], sends.at[2, 0], recvs.at[2, 0], {"space": beside})
    copy.start()
    w_beside.append(copy)
    upward = remote(
        acts.at[depth - 1],
        halo.at[0],
        sends.at[5, 0],
        recvs.at[5, 0],
        {"space": lax.rem(me + 1, parts)},
    )
    downward = remote(
        acts.at[0],
        halo.at[1],
        sends.at[5, 1],
        recvs.at[5, 1],
        {"space": lax.rem(me + parts - 1, parts)},
    )

    at_z = lax.broadcasted_iota(jnp.int32, (half_y, half_z, channels), 1).reshape(small, channels)

    def spread(x, carry):
        values[x] = pre[x].astype(f32).reshape(half_y, 2, height, channels)
        for odd_y in (0, 1):
            pair = []
            for odd_z in (0, 1):
                cells = values[x, :, odd_y, pl.ds(odd_z, half_z, stride=2), :]
                cells = cells.reshape(small, channels)
                pair.append(jnp.where(cells > 0, cells, leak_slope * cells))
            earlier = jnp.where(at_z == 0, 0.0, pltpu.roll(pair[1], 1, 0))
            row = half_z * odd_y
            thin[x, odd_y, pl.ds(row, small), 0:channels] = earlier.astype(bf16)
            thin[x, odd_y, pl.ds(row, small), channels : 2 * channels] = pair[0].astype(bf16)
            thin[x, odd_y, pl.ds(row, small), 2 * channels :] = pair[1].astype(bf16)
        thin[x, 1, 0:half_z, :] = jnp.zeros((half_z, 3 * channels), bf16)
        return carry

    load_pre.wait()
    lax.fori_loop(0, depth, spread, 0)

    at_cell = lax.broadcasted_iota(jnp.int32, (across, height, channels), 1)
    at_cell = at_cell.reshape(plane, channels)

    def place(q, cells):
        cells = cells.astype(f32)
        inner = pl.ds(height, plane)
        earlier = jnp.where(at_cell == 0, 0.0, pltpu.roll(cells, 1, 0))
        later = jnp.where(at_cell == height - 1, 0.0, pltpu.roll(cells, plane - 1, 0))
        frame[q, inner, 0:channels] = earlier.astype(bf16)
        frame[q, inner, channels : 2 * channels] = cells.astype(bf16)
        frame[q, inner, 2 * channels :] = later.astype(bf16)
        nothing = jnp.zeros((height, 3 * channels), bf16)
        frame[q, 0:height, :] = nothing
        frame[q, pl.ds(height + plane, height), :] = nothing

    def place_own(x, carry):
        place(x + 1, acts[x])
        return carry

    load_acts.wait()
    lax.fori_loop(0, depth, place_own, 0)

    def take_cotangents(s, block):
        start = pl.multiple_of(s * rows, rows)
        g_turned[:, pl.ds(start, rows), :] = block.astype(f32)

    take_cotangents(me, g_send[pl.ds(me * half_x, half_x + 1)])
    for d in range(1, parts):
        g_copies[d - 1].wait_recv()
        take_cotangents(lax.rem(me + parts - d, parts), gbuf[d - 1])
    for p in range(half_x + 1):
        g_mixed[p] = g_turned[p].T
        for y in range(half_y):
            cells = g_mixed[p, pl.ds(y, half_z, stride=half_y), :]
            g_cells[p, y * half_z : (y + 1) * half_z, :] = cells
        g_turned[p] = g_cells[p].T

    for i in range(1, parts // 2):
        w_copies[i - 1].wait_recv()
        block = wbuf.at[0, i, core]
        copy = remote(block, wbuf.at[1, i, core], sends.at[2, i], recvs.at[2, i], {"space": beside})
        copy.start()
        w_beside.append(copy)
        copy = remote(block, block, sends.at[3, i], recvs.at[3, i], {"dp": partner})
        copy.start()
        forwards.append((0, i, copy))
    for tap_x in range(3):
        for tap_y in range(3):
            total = None
            for p in range(half_x):
                at_p, at_x = (p + 1, 2 * p + 1) if tap_x == 0 else (p, 2 * p + tap_x - 1)
                lhs = g_turned[at_p].astype(bf16)
                row = half_z if tap_y == 2 else 0
                rhs = thin[at_x, 0 if tap_y == 1 else 1, row : row + small, :]
                term = jnp.dot(lhs, rhs, preferred_element_type=f32)
                total = term if total is None else total + term
            for tap_z in range(3):
                coarse[9 * tap_x + 3 * tap_y + tap_z] = total[
                    :, tap_z * channels : (tap_z + 1) * channels
                ]
    for u in range(27, coarse.shape[0]):
        coarse[u] = jnp.zeros((channels, channels), f32)
    coarse_sum.to_core()
    for i in range(parts // 2):
        w_beside[i].wait_recv()
        block = wbuf.at[1, i, core]
        copy = remote(block, block, sends.at[4, i], recvs.at[4, i], {"dp": partner})
        copy.start()
        forwards.append((1, i, copy))
    pl.when(me < parts - 1)(upward.start)
    pl.when(me > 0)(downward.start)

    for p in range(half_x + 1):
        cells = g_cells[p]
        later = jnp.where(at_z == half_z - 1, 0.0, pltpu.roll(cells, small - 1, 0))
        g_rows[p, 0:small, 0:channels] = cells.astype(bf16)
        g_rows[p, 0:small, channels:] = later.astype(bf16)
        g_rows[p, small : small + half_z, :] = jnp.zeros((half_z, 2 * channels), bf16)

    def take_filters(s, part, block):
        start = pl.multiple_of(s * rows, rows)
        w_full[pl.ds(part * (half - 1), half), pl.ds(start, rows), :] = block.astype(f32)

    for part in (0, 1):
        take_filters(me, part, w_ref[part * (half - 1) : part * (half - 1) + half])
    for side, i, copy in forwards:
        copy.wait_recv()
        source = beside if side else me
        for part in (0, 1):
            take_filters(lax.rem(source + parts - 2 * i, parts), part, wbuf[side, i, part])

    def mix(t, carry):
        mixing[t, 0:channels, 0:channels] = w_full[3 * t + 1].astype(bf16)
        mixing[t, 0:channels, channels:] = w_full[3 * t + 2].astype(bf16)
        mixing[t, channels:, 0:channels] = jnp.zeros((channels, channels), bf16)
        mixing[t, channels:, channels:] = w_full[3 * t].astype(bf16)
        return carry

    lax.fori_loop(0, 9, mix, 0)
    coarse_sum.to_chips()

    def propagate(p, carry):
        for odd_x in (0, 1):
            for odd_y in (0, 1):
                total = None
                for tap_x, move_x in parity_taps[odd_x]:
                    for tap_y, move_y in parity_taps[odd_y]:
                        cells = g_rows[p + move_x, move_y * half_z : move_y * half_z + small, :]
                        term = jnp.dot(
                            cells, mixing[3 * tap_x + tap_y], preferred_element_type=f32
                        )
                        total = term if total is None else total + term
                for odd_z in (0, 1):
                    where = (2 * p + odd_x, slice(None), odd_y, pl.ds(odd_z, half_z, stride=2))
                    before = values[where].reshape(small, channels)
                    piece = total[:, odd_z * channels : (odd_z + 1) * channels]
                    piece = piece * jnp.where(before > 0, 1.0, leak_slope)
                    values[where] = piece.reshape(half_y, half_z, channels)
        for odd_x in (0, 1):
            x = 2 * p + odd_x
            cells = values[x].reshape(plane, channels)
            delta[pl.ds(pl.multiple_of(x * channels, channels), channels), :] = cells.T.astype(bf16)
        return carry

    lax.fori_loop(0, half_x, propagate, 0)

    def clear(u, carry):
        outer[u] = jnp.zeros((channels, channels), f32)
        return carry

    lax.fori_loop(0, outer.shape[0], clear, 0)
    for u in range(middle.shape[0]):
        middle[u] = jnp.zeros((channels, channels), f32)

    def layer(q):
        low, high = max(0, q - 2), min(depth - 1, q)

        slabs = [frame[q, y * height : y * height + plane, :] for y in range(3)]
        lhs = delta[low * channels : (high + 1) * channels, :]
        total = jnp.dot(lhs, jnp.concatenate(slabs, axis=1), preferred_element_type=f32)
        for x in range(low, high + 1):
            into, first = (middle, 0) if q - x == 1 else (outer, 9 * ((q - x) // 2))
            for tap in range(9):
                into[first + tap] += total[
                    (x - low) * channels : (x - low + 1) * channels,
                    tap * channels : (tap + 1) * channels,
                ]

    layer(1)
    coarse_sum.to_space()
    for q in range(2, depth):
        layer(q)
    coarse_sum.to_copies()
    layer(depth)

    middle_sum.to_core()

    @pl.when(me > 0)
    def _():
        upward.wait_recv()
        place(0, halo[0])
        layer(0)

    middle_sum.to_chips()

    @pl.when(me < parts - 1)
    def _():
        downward.wait_recv()
        place(depth + 1, halo[1])
        layer(depth + 1)

    outer_sum.to_core()
    middle_sum.to_space()
    outer_sum.to_chips()
    coarse_sum.finish()
    middle_sum.to_copies()
    outer_sum.to_space()
    middle_sum.finish()
    outer_sum.to_copies()
    outer_sum.finish()
    for copy in g_copies + w_copies + w_beside + [copy for _, _, copy in forwards]:
        copy.wait_send()
    pl.when(me < parts - 1)(upward.wait_send)
    pl.when(me > 0)(downward.wait_send)


def reduction_scratch(dp, parts, channels, taps):
    chunk = -(-taps // dp)
    ranks = dp // 2
    rows = channels // parts
    most = max(dp, parts)
    return [
        VMEM((chunk * dp, channels, channels), f32),
        VMEM((ranks, chunk, channels, channels), f32),
        VMEM((ranks - 1, chunk, channels, channels), bf16),
        VMEM((ranks - 1, chunk, channels, channels), bf16),
        VMEM((parts - 1, chunk * rows, channels), bf16),
        VMEM((parts - 1, chunk * rows, channels), bf16),
        VMEM((dp, chunk * rows, channels), f32),
        pltpu.SemaphoreType.DMA((4, most)),
        pltpu.SemaphoreType.DMA((4, most)),
    ]


def gradients(dp, parts, scaling, sizes, acts, pre, w, g):
    depth, across, height, channels = sizes
    half_x, half_y, half_z = depth // 2, across // 2, height // 2
    plane, small = across * height, half_y * half_z
    chunk = -(-27 // dp)
    rows = channels // parts
    half = (w.shape[0] + 1) // 2
    units = [chunk * dp]
    for taps, where in ((9, middle_place), (18, outer_place)):
        units.append(where(-(-taps // dp) * dp - 1) + 1)
    flops = 2 * 27 * channels * channels * (depth * plane + 2 * half_x * small)
    return pl.pallas_call(
        functools.partial(kernel, dp, parts, scaling, sizes),
        out_shape=[
            jax.ShapeDtypeStruct((n, rows, channels), f32) for n in (units[0], max(units[1:]))
        ],
        in_specs=[pl.BlockSpec(memory_space=pl.ANY)] * 2 + [pl.BlockSpec(memory_space=VMEM)] * 2,
        out_specs=[pl.BlockSpec(memory_space=VMEM)] * 2,
        scratch_shapes=reduction_scratch(dp, parts, channels, 27)
        + reduction_scratch(dp, parts, channels, 9)
        + reduction_scratch(dp, parts, channels, 18)
        + [
            VMEM((2, parts // 2, 2, half, rows, channels), bf16),
            VMEM((parts - 1, half_x + 1, rows, small), bf16),
            VMEM((2, plane, channels), bf16),
            pltpu.SemaphoreType.DMA((6, parts)),
            pltpu.SemaphoreType.DMA((6, parts)),
            VMEM((27, channels, channels), f32),
            VMEM((9, 2 * channels, 2 * channels), bf16),
            VMEM((g.shape[0] + 1, rows, small), bf16),
            VMEM((half_x + 1, channels, small), f32),
            VMEM((half_x + 1, small, channels), f32),
            VMEM((half_x + 1, small, channels), f32),
            VMEM((half_x + 1, small + half_z, 2 * channels), bf16),
            VMEM((depth, half_y, 2, height, channels), f32),
            VMEM((depth, 2, small + half_z, 3 * channels), bf16),
            VMEM((depth + 2, plane + 2 * height, 3 * channels), bf16),
            VMEM((depth * channels, plane), bf16),
            VMEM((depth, plane, channels), bf16),
            VMEM((depth, plane, channels), bf16),
            pltpu.SemaphoreType.DMA((2,)),
        ],
        cost_estimate=pl.CostEstimate(flops=flops, bytes_accessed=8 << 20, transcendentals=0),
        compiler_params=pltpu.CompilerParams(
            collective_id=0, has_side_effects=True, vmem_limit_bytes=56 << 20
        ),
    )(acts, pre, w, g)


def body(acts_in, pre_act, weight_two, grad_out):
    parts = lax.axis_size("space")
    groups = lax.axis_size("dp")
    depth, across, height, channels = sizes = acts_in.shape[1:]
    rows = weight_two.shape[0]
    scaling = 1.0 / math.sqrt(groups * depth * parts * across * height)
    turned = grad_out[0].transpose(0, 2, 3, 1)
    shard = weight_two.reshape(rows, 27, channels).transpose(1, 0, 2)
    flat = (depth, across * height, channels)
    coarse, fine = gradients(
        groups, parts, scaling, sizes, acts_in.reshape(flat), pre_act.reshape(flat), shard, turned
    )

    def by_filter(totals):
        taps = totals[:27]
        return taps.transpose(1, 0, 2).reshape(rows, 3, 3, 3, channels)

    return (by_filter(fine), by_filter(coarse))


def solution(mesh):
    placed = (
        P("dp", "space", None, None, None),
        P("dp", "space", None, None, None),
        P("space", None, None, None, None),
        P("dp", None, None, None, "space"),
    )
    return jax.shard_map(
        body,
        mesh=mesh,
        in_specs=placed,
        out_specs=(P("space", None, None, None, None), P("space", None, None, None, None)),
        check_vma=False,
    )
```

```python
import functools
import math

import jax
import jax.numpy as jnp
from jax import lax
from jax.experimental import pallas as pl
from jax.experimental.pallas import tpu as pltpu
from jax.sharding import PartitionSpec as P

leak_slope = 0.3
parity_taps = {0: ((1, 0),), 1: ((0, 1), (2, 0))}
MESH = pl.DeviceIdType.MESH
VMEM = pltpu.VMEM
f32, bf16 = jnp.float32, jnp.bfloat16


def remote(src, dst, send, recv, target):
    return pltpu.make_async_remote_copy(
        src_ref=src,
        dst_ref=dst,
        send_sem=send,
        recv_sem=recv,
        device_id=target,
        device_id_type=MESH,
    )


def hello(dp, parts):
    me, mine = lax.axis_index("space"), lax.axis_index("dp")
    barrier = pltpu.get_barrier_semaphore()
    for d in range(1, parts):
        pl.semaphore_signal(
            barrier, inc=1, device_id={"space": lax.rem(me + d, parts)}, device_id_type=MESH
        )
    for d in range(1, dp):
        pl.semaphore_signal(
            barrier, inc=1, device_id={"dp": lax.rem(mine + d, dp)}, device_id_type=MESH
        )


class Reduction:
    def __init__(self, dp, parts, scaling, out, place, part, scratch):
        self.place = place
        self.dp, self.parts, self.scaling, self.out, self.part = dp, parts, scaling, out, part
        self.got, self.away, self.came, self.apart, self.near, self.whole, self.sends, self.recvs = scratch
        self.me, self.mine = lax.axis_index("space"), lax.axis_index("dp")
        self.core = lax.rem(self.mine, 2)
        self.rest = self.mine // 2
        self.ranks = dp // 2
        self.chunk = part.shape[0] // dp
        self.half = self.chunk * self.ranks
        self.order = list(range(1, self.ranks)) + [0]
        self.rows = part.shape[1] // parts
        self.inputs = part.shape[2]

    def to_core(self):
        self.first = []
        theirs = (1 - self.core) * self.half
        for d in self.order:
            j = lax.rem(self.rest + d, self.ranks)
            copy = remote(
                self.part.at[pl.ds(theirs + j * self.chunk, self.chunk)],
                self.got.at[d],
                self.sends.at[0, d],
                self.recvs.at[0, d],
                {"dp": self.mine + 1 - 2 * self.core},
            )
            copy.start()
            self.first.append(copy)

    def to_chips(self):
        self.second = []
        for d, copy in zip(self.order, self.first):
            j = lax.rem(self.rest + d, self.ranks)
            base = self.core * self.half + j * self.chunk
            copy.wait_recv()
            if d:

                def fill(u, carry):
                    self.away[d - 1, u] = (self.part[base + u] + self.got[d, u]).astype(bf16)
                    return carry

                lax.fori_loop(0, self.chunk, fill, 0)
                onward = remote(
                    self.away.at[d - 1],
                    self.came.at[d - 1],
                    self.sends.at[1, d],
                    self.recvs.at[1, d],
                    {"dp": 2 * j + self.core},
                )
                onward.start()
                self.second.append(onward)

    def to_space(self):
        base = self.core * self.half + self.rest * self.chunk
        for onward in self.second:
            onward.wait_recv()

        def settle(u, carry):
            total = self.part[base + u] + self.got[0, u]
            for d in range(1, self.ranks):
                total = total + self.came[d - 1, u].astype(f32)
            self.got[0, u] = total
            return carry

        lax.fori_loop(0, self.chunk, settle, 0)
        self.third = []
        for d in range(1, self.parts):
            t = lax.rem(self.me + d, self.parts)
            self.apart[d - 1] = self.block(t).astype(bf16)
            copy = remote(
                self.apart.at[d - 1],
                self.near.at[d - 1],
                self.sends.at[2, d],
                self.recvs.at[2, d],
                {"space": t},
            )
            copy.start()
            self.third.append(copy)

    def block(self, t):
        start = pl.multiple_of(t * self.rows, self.rows)
        taps = self.got[0, :, pl.ds(start, self.rows), :]
        return taps.reshape(self.chunk * self.rows, self.inputs)

    def to_copies(self):
        total = self.block(self.me)
        for d in range(1, self.parts):
            self.third[d - 1].wait_recv()
            total = total + self.near[d - 1].astype(f32)
        self.whole[0] = total * self.scaling
        self.fourth = []
        for d in range(1, self.dp):
            copy = remote(
                self.whole.at[0],
                self.whole.at[d],
                self.sends.at[3, d],
                self.recvs.at[3, d],
                {"dp": lax.rem(self.mine + d, self.dp)},
            )
            copy.start()
            self.fourth.append(copy)

    def put(self, c, d):
        for u in range(self.chunk):
            taps = self.whole[d, u * self.rows : (u + 1) * self.rows, :]
            self.out[self.place(c * self.chunk + u)] = taps

    def finish(self):
        self.put(self.core * self.ranks + self.rest, 0)
        for d in range(1, self.dp):
            self.fourth[d - 1].wait_recv()
            other = lax.rem(self.mine + self.dp - d, self.dp)
            self.put(lax.rem(other, 2) * self.ranks + other // 2, d)
        for copy in self.first + self.second + self.third + self.fourth:
            copy.wait_send()


def place_of(tap_x):
    return lambda u: 9 * tap_x + u + 27 * (u // 9)


def kernel(dp, parts, scaling, sizes, acts_far, pre_far, w_ref, g_ref, coarse_out, fine_out, *scratch):
    coarse, fine = scratch[0], [scratch[9 * n + 9] for n in range(3)]
    share = (dp, parts, scaling)
    coarse_sum = Reduction(*share, coarse_out, lambda u: u, coarse, scratch[1:9])
    fine_sum = []
    for n in range(3):
        own = scratch[9 * n + 10 : 9 * n + 18]
        fine_sum.append(Reduction(*share, fine_out, place_of(n), fine[n], own))
    (wbuf, gbuf, halo, sends, recvs, w_full, mixing, g_send, g_turned, g_mixed, g_cells, g_rows, values, thin, frame, delta, acts, pre, loads) = scratch[36:]
    depth, across, height, channels = sizes
    half_x, half_y, half_z = depth // 2, across // 2, height // 2
    plane, small = across * height, half_y * half_z
    rows = channels // parts
    me, mine = lax.axis_index("space"), lax.axis_index("dp")
    core = lax.rem(mine, 2)
    partner = mine + 1 - 2 * core
    half = (w_ref.shape[0] + 1) // 2
    beside = me + 1 - 2 * lax.rem(me, 2)
    hello(dp, parts)
    load_pre = pltpu.make_async_copy(pre_far, pre, loads.at[0])
    load_acts = pltpu.make_async_copy(acts_far, acts, loads.at[1])
    load_pre.start()
    load_acts.start()

    count = 128 // half_y

    def pack(x, carry):
        for group in range(half_z // count):
            cells = [g_ref[x, group * count + j].astype(f32) for j in range(count)]
            g_send[x, :, group * 128 : (group + 1) * 128] = jnp.concatenate(cells, axis=1).astype(bf16)
        return carry

    lax.fori_loop(0, g_ref.shape[0], pack, 0)
    g_send[g_ref.shape[0]] = jnp.zeros((rows, small), bf16)
    pl.semaphore_wait(pltpu.get_barrier_semaphore(), parts + dp - 2)

    g_copies, w_copies, w_beside, forwards = [], [], [], []
    for d in range(1, parts):
        t = lax.rem(me + d, parts)
        mine_there = g_send.at[pl.ds(t * half_x, half_x + 1)]
        copy = remote(mine_there, gbuf.at[d - 1], sends.at[0, d], recvs.at[0, d], {"space": t})
        copy.start()
        g_copies.append(copy)
    own = w_ref.at[pl.ds(core * (half - 1), half)]
    for i in range(1, parts // 2):
        t = lax.rem(me + 2 * i, parts)
        copy = remote(own, wbuf.at[0, i, core], sends.at[1, i], recvs.at[1, i], {"space": t})
        copy.start()
        w_copies.append(copy)
    copy = remote(own, wbuf.at[1, 0, core], sends.at[2, 0], recvs.at[2, 0], {"space": beside})
    copy.start()
    w_beside.append(copy)
    upward = remote(
        acts.at[depth - 1],
        halo.at[0],
        sends.at[5, 0],
        recvs.at[5, 0],
        {"space": lax.rem(me + 1, parts)},
    )
    downward = remote(
        acts.at[0],
        halo.at[1],
        sends.at[5, 1],
        recvs.at[5, 1],
        {"space": lax.rem(me + parts - 1, parts)},
    )

    at_z = lax.broadcasted_iota(jnp.int32, (half_y, half_z, channels), 1).reshape(small, channels)

    def spread(x, carry):
        values[x] = pre[x].astype(f32).reshape(half_y, 2, height, channels)
        for odd_y in (0, 1):
            pair = []
            for odd_z in (0, 1):
                cells = values[x, :, odd_y, pl.ds(odd_z, half_z, stride=2), :]
                cells = cells.reshape(small, channels)
                pair.append(jnp.where(cells > 0, cells, leak_slope * cells))
            earlier = jnp.where(at_z == 0, 0.0, pltpu.roll(pair[1], 1, 0))
            row = half_z * odd_y
            thin[x, odd_y, pl.ds(row, small), 0:channels] = earlier.astype(bf16)
            thin[x, odd_y, pl.ds(row, small), channels : 2 * channels] = pair[0].astype(bf16)
            thin[x, odd_y, pl.ds(row, small), 2 * channels :] = pair[1].astype(bf16)
        thin[x, 1, 0:half_z, :] = jnp.zeros((half_z, 3 * channels), bf16)
        return carry

    load_pre.wait()
    lax.fori_loop(0, depth, spread, 0)

    at_cell = lax.broadcasted_iota(jnp.int32, (across, height, channels), 1)
    at_cell = at_cell.reshape(plane, channels)

    def place(q, cells):
        cells = cells.astype(f32)
        inner = pl.ds(height, plane)
        earlier = jnp.where(at_cell == 0, 0.0, pltpu.roll(cells, 1, 0))
        later = jnp.where(at_cell == height - 1, 0.0, pltpu.roll(cells, plane - 1, 0))
        frame[q, inner, 0:channels] = earlier.astype(bf16)
        frame[q, inner, channels : 2 * channels] = cells.astype(bf16)
        frame[q, inner, 2 * channels :] = later.astype(bf16)
        nothing = jnp.zeros((height, 3 * channels), bf16)
        frame[q, 0:height, :] = nothing
        frame[q, pl.ds(height + plane, height), :] = nothing

    def place_own(x, carry):
        place(x + 1, acts[x])
        return carry

    load_acts.wait()
    lax.fori_loop(0, depth, place_own, 0)

    def take_cotangents(s, block):
        start = pl.multiple_of(s * rows, rows)
        g_turned[:, pl.ds(start, rows), :] = block.astype(f32)

    take_cotangents(me, g_send[pl.ds(me * half_x, half_x + 1)])
    for d in range(1, parts):
        g_copies[d - 1].wait_recv()
        take_cotangents(lax.rem(me + parts - d, parts), gbuf[d - 1])
    for p in range(half_x + 1):
        g_mixed[p] = g_turned[p].T
        for y in range(half_y):
            cells = g_mixed[p, pl.ds(y, half_z, stride=half_y), :]
            g_cells[p, y * half_z : (y + 1) * half_z, :] = cells
        g_turned[p] = g_cells[p].T

    for i in range(1, parts // 2):
        w_copies[i - 1].wait_recv()
        block = wbuf.at[0, i, core]
        copy = remote(block, wbuf.at[1, i, core], sends.at[2, i], recvs.at[2, i], {"space": beside})
        copy.start()
        w_beside.append(copy)
        copy = remote(block, block, sends.at[3, i], recvs.at[3, i], {"dp": partner})
        copy.start()
        forwards.append((0, i, copy))
    for tap_x in range(3):
        for tap_y in range(3):
            total = None
            for p in range(half_x):
                at_p, at_x = (p + 1, 2 * p + 1) if tap_x == 0 else (p, 2 * p + tap_x - 1)
                lhs = g_turned[at_p].astype(bf16)
                row = half_z if tap_y == 2 else 0
                rhs = thin[at_x, 0 if tap_y == 1 else 1, row : row + small, :]
                term = jnp.dot(lhs, rhs, preferred_element_type=f32)
                total = term if total is None else total + term
            for tap_z in range(3):
                coarse[9 * tap_x + 3 * tap_y + tap_z] = total[
                    :, tap_z * channels : (tap_z + 1) * channels
                ]
    for u in range(27, coarse.shape[0]):
        coarse[u] = jnp.zeros((channels, channels), f32)
    coarse_sum.to_core()
    for i in range(parts // 2):
        w_beside[i].wait_recv()
        block = wbuf.at[1, i, core]
        copy = remote(block, block, sends.at[4, i], recvs.at[4, i], {"dp": partner})
        copy.start()
        forwards.append((1, i, copy))
    pl.when(me < parts - 1)(upward.start)

    for p in range(half_x + 1):
        cells = g_cells[p]
        later = jnp.where(at_z == half_z - 1, 0.0, pltpu.roll(cells, small - 1, 0))
        g_rows[p, 0:small, 0:channels] = cells.astype(bf16)
        g_rows[p, 0:small, channels:] = later.astype(bf16)
        g_rows[p, small : small + half_z, :] = jnp.zeros((half_z, 2 * channels), bf16)

    def take_filters(s, part, block):
        start = pl.multiple_of(s * rows, rows)
        w_full[pl.ds(part * (half - 1), half), pl.ds(start, rows), :] = block.astype(f32)

    for part in (0, 1):
        take_filters(me, part, w_ref[part * (half - 1) : part * (half - 1) + half])
    for side, i, copy in forwards:
        copy.wait_recv()
        source = beside if side else me
        for part in (0, 1):
            take_filters(lax.rem(source + parts - 2 * i, parts), part, wbuf[side, i, part])

    def mix(t, carry):
        mixing[t, 0:channels, 0:channels] = w_full[3 * t + 1].astype(bf16)
        mixing[t, 0:channels, channels:] = w_full[3 * t + 2].astype(bf16)
        mixing[t, channels:, 0:channels] = jnp.zeros((channels, channels), bf16)
        mixing[t, channels:, channels:] = w_full[3 * t].astype(bf16)
        return carry

    lax.fori_loop(0, 9, mix, 0)
    coarse_sum.to_chips()

    def propagate(p, carry):
        for odd_x in (0, 1):
            for odd_y in (0, 1):
                total = None
                for tap_x, move_x in parity_taps[odd_x]:
                    for tap_y, move_y in parity_taps[odd_y]:
                        cells = g_rows[p + move_x, move_y * half_z : move_y * half_z + small, :]
                        term = jnp.dot(
                            cells, mixing[3 * tap_x + tap_y], preferred_element_type=f32
                        )
                        total = term if total is None else total + term
                for odd_z in (0, 1):
                    where = (2 * p + odd_x, slice(None), odd_y, pl.ds(odd_z, half_z, stride=2))
                    before = values[where].reshape(small, channels)
                    piece = total[:, odd_z * channels : (odd_z + 1) * channels]
                    piece = piece * jnp.where(before > 0, 1.0, leak_slope)
                    values[where] = piece.reshape(half_y, half_z, channels)
        for odd_x in (0, 1):
            x = 2 * p + odd_x
            cells = values[x].reshape(plane, channels).astype(bf16)
            delta[pl.ds(pl.multiple_of(x * channels, channels), channels), :] = cells.T
        return carry

    lax.fori_loop(0, half_x, propagate, 0)
    pl.when(me > 0)(downward.start)

    for tap_x in range(3):
        for u in range(fine[tap_x].shape[0]):
            fine[tap_x][u] = jnp.zeros((channels, channels), f32)

    def layer(q):
        low, high = max(0, q - 2), min(depth - 1, q)

        slabs = [frame[q, y * height : y * height + plane, :] for y in range(3)]
        lhs = delta[low * channels : (high + 1) * channels, :]
        total = jnp.dot(lhs, jnp.concatenate(slabs, axis=1), preferred_element_type=f32)
        for x in range(low, high + 1):
            for tap in range(9):
                fine[q - x][tap] += total[
                    (x - low) * channels : (x - low + 1) * channels,
                    tap * channels : (tap + 1) * channels,
                ]

    layer(1)
    coarse_sum.to_space()
    for q in range(2, depth):
        layer(q)
    coarse_sum.to_copies()

    @pl.when(me > 0)
    def _():
        upward.wait_recv()
        place(0, halo[0])
        layer(0)

    fine_sum[0].to_core()
    layer(depth)
    fine_sum[1].to_core()
    fine_sum[0].to_chips()

    @pl.when(me < parts - 1)
    def _():
        downward.wait_recv()
        place(depth + 1, halo[1])
        layer(depth + 1)

    fine_sum[2].to_core()
    fine_sum[1].to_chips()
    fine_sum[0].to_space()
    fine_sum[2].to_chips()
    fine_sum[1].to_space()
    coarse_sum.finish()
    fine_sum[0].to_copies()
    fine_sum[2].to_space()
    fine_sum[1].to_copies()
    fine_sum[0].finish()
    fine_sum[1].finish()
    fine_sum[2].to_copies()
    fine_sum[2].finish()
    for copy in g_copies + w_copies + w_beside + [copy for _, _, copy in forwards]:
        copy.wait_send()
    pl.when(me < parts - 1)(upward.wait_send)
    pl.when(me > 0)(downward.wait_send)


def reduction_scratch(dp, parts, channels, taps):
    chunk = -(-taps // dp)
    ranks = dp // 2
    rows = channels // parts
    most = max(dp, parts)
    return [
        VMEM((chunk * dp, channels, channels), f32),
        VMEM((ranks, chunk, channels, channels), f32),
        VMEM((ranks - 1, chunk, channels, channels), bf16),
        VMEM((ranks - 1, chunk, channels, channels), bf16),
        VMEM((parts - 1, chunk * rows, channels), bf16),
        VMEM((parts - 1, chunk * rows, channels), bf16),
        VMEM((dp, chunk * rows, channels), f32),
        pltpu.SemaphoreType.DMA((4, most)),
        pltpu.SemaphoreType.DMA((4, most)),
    ]


def gradients(dp, parts, scaling, sizes, acts, pre, w, g):
    depth, across, height, channels = sizes
    half_x, half_y, half_z = depth // 2, across // 2, height // 2
    plane, small = across * height, half_y * half_z
    chunk = -(-27 // dp)
    rows = channels // parts
    half = (w.shape[0] + 1) // 2
    units = [chunk * dp, place_of(2)(-(-9 // dp) * dp - 1) + 1]
    flops = 2 * 27 * channels * channels * (depth * plane + 2 * half_x * small)
    return pl.pallas_call(
        functools.partial(kernel, dp, parts, scaling, sizes),
        out_shape=[
            jax.ShapeDtypeStruct((n, rows, channels), f32) for n in units
        ],
        in_specs=[pl.BlockSpec(memory_space=pl.ANY)] * 2 + [pl.BlockSpec(memory_space=VMEM)] * 2,
        out_specs=[pl.BlockSpec(memory_space=VMEM)] * 2,
        scratch_shapes=reduction_scratch(dp, parts, channels, 27)
        + reduction_scratch(dp, parts, channels, 9) * 3
        + [
            VMEM((2, parts // 2, 2, half, rows, channels), bf16),
            VMEM((parts - 1, half_x + 1, rows, small), bf16),
            VMEM((2, plane, channels), bf16),
            pltpu.SemaphoreType.DMA((6, parts)),
            pltpu.SemaphoreType.DMA((6, parts)),
            VMEM((27, channels, channels), f32),
            VMEM((9, 2 * channels, 2 * channels), bf16),
            VMEM((g.shape[0] + 1, rows, small), bf16),
            VMEM((half_x + 1, channels, small), f32),
            VMEM((half_x + 1, small, channels), f32),
            VMEM((half_x + 1, small, channels), f32),
            VMEM((half_x + 1, small + half_z, 2 * channels), bf16),
            VMEM((depth, half_y, 2, height, channels), f32),
            VMEM((depth, 2, small + half_z, 3 * channels), bf16),
            VMEM((depth + 2, plane + 2 * height, 3 * channels), bf16),
            VMEM((depth * channels, plane), bf16),
            VMEM((depth, plane, channels), bf16),
            VMEM((depth, plane, channels), bf16),
            pltpu.SemaphoreType.DMA((2,)),
        ],
        cost_estimate=pl.CostEstimate(flops=flops, bytes_accessed=8 << 20, transcendentals=0),
        compiler_params=pltpu.CompilerParams(
            collective_id=0, has_side_effects=True, vmem_limit_bytes=56 << 20
        ),
    )(acts, pre, w, g)


def body(acts_in, pre_act, weight_two, grad_out):
    parts = lax.axis_size("space")
    groups = lax.axis_size("dp")
    depth, across, height, channels = sizes = acts_in.shape[1:]
    rows = weight_two.shape[0]
    scaling = 1.0 / math.sqrt(groups * depth * parts * across * height)
    turned = grad_out[0].transpose(0, 2, 3, 1)
    shard = weight_two.reshape(rows, 27, channels).transpose(1, 0, 2)
    flat = (depth, across * height, channels)
    coarse, fine = gradients(
        groups, parts, scaling, sizes, acts_in.reshape(flat), pre_act.reshape(flat), shard, turned
    )

    def by_filter(totals):
        taps = totals[:27]
        return taps.transpose(1, 0, 2).reshape(rows, 3, 3, 3, channels)

    return (by_filter(fine), by_filter(coarse))


def solution(mesh):
    placed = (
        P("dp", "space", None, None, None),
        P("dp", "space", None, None, None),
        P("space", None, None, None, None),
        P("dp", None, None, None, "space"),
    )
    return jax.shard_map(
        body,
        mesh=mesh,
        in_specs=placed,
        out_specs=(P("space", None, None, None, None), P("space", None, None, None, None)),
        check_vma=False,
    )
```

```python
import functools
import math

import jax
import jax.numpy as jnp
from jax import lax
from jax.experimental import pallas as pl
from jax.experimental.pallas import tpu as pltpu
from jax.sharding import PartitionSpec as P

leak_slope = 0.3
parity_taps = {0: ((1, 0),), 1: ((0, 1), (2, 0))}
MESH = pl.DeviceIdType.MESH
VMEM = pltpu.VMEM
f32, bf16 = jnp.float32, jnp.bfloat16


def remote(src, dst, send, recv, target):
    return pltpu.make_async_remote_copy(
        src_ref=src,
        dst_ref=dst,
        send_sem=send,
        recv_sem=recv,
        device_id=target,
        device_id_type=MESH,
    )


def hello(dp, parts):
    me, mine = lax.axis_index("space"), lax.axis_index("dp")
    barrier = pltpu.get_barrier_semaphore()
    for d in range(1, parts):
        pl.semaphore_signal(
            barrier, inc=1, device_id={"space": lax.rem(me + d, parts)}, device_id_type=MESH
        )
    for d in range(1, dp):
        pl.semaphore_signal(
            barrier, inc=1, device_id={"dp": lax.rem(mine + d, dp)}, device_id_type=MESH
        )


class Reduction:
    def __init__(self, dp, parts, scaling, out, place, part, scratch):
        self.place = place
        self.dp, self.parts, self.scaling, self.out, self.part = dp, parts, scaling, out, part
        self.got, self.away, self.came, self.apart, self.near, self.whole, self.sends, self.recvs = scratch
        self.me, self.mine = lax.axis_index("space"), lax.axis_index("dp")
        self.core = lax.rem(self.mine, 2)
        self.rest = self.mine // 2
        self.ranks = dp // 2
        self.chunk = part.shape[0] // dp
        self.half = self.chunk * self.ranks
        self.order = list(range(1, self.ranks)) + [0]
        self.rows = part.shape[1] // parts
        self.inputs = part.shape[2]

    def to_core(self):
        self.first = []
        theirs = (1 - self.core) * self.half
        for d in self.order:
            j = lax.rem(self.rest + d, self.ranks)
            copy = remote(
                self.part.at[pl.ds(theirs + j * self.chunk, self.chunk)],
                self.got.at[d],
                self.sends.at[0, d],
                self.recvs.at[0, d],
                {"dp": self.mine + 1 - 2 * self.core},
            )
            copy.start()
            self.first.append(copy)

    def to_chips(self):
        self.second = []
        for d, copy in zip(self.order, self.first):
            j = lax.rem(self.rest + d, self.ranks)
            base = self.core * self.half + j * self.chunk
            copy.wait_recv()
            if d:

                def fill(u, carry):
                    self.away[d - 1, u] = (self.part[base + u] + self.got[d, u]).astype(bf16)
                    return carry

                lax.fori_loop(0, self.chunk, fill, 0)
                onward = remote(
                    self.away.at[d - 1],
                    self.came.at[d - 1],
                    self.sends.at[1, d],
                    self.recvs.at[1, d],
                    {"dp": 2 * j + self.core},
                )
                onward.start()
                self.second.append(onward)

    def to_space(self):
        base = self.core * self.half + self.rest * self.chunk
        for onward in self.second:
            onward.wait_recv()

        def settle(u, carry):
            total = self.part[base + u] + self.got[0, u]
            for d in range(1, self.ranks):
                total = total + self.came[d - 1, u].astype(f32)
            self.got[0, u] = total
            return carry

        lax.fori_loop(0, self.chunk, settle, 0)
        self.third = []
        for d in range(1, self.parts):
            t = lax.rem(self.me + d, self.parts)
            self.apart[d - 1] = self.block(t).astype(bf16)
            copy = remote(
                self.apart.at[d - 1],
                self.near.at[d - 1],
                self.sends.at[2, d],
                self.recvs.at[2, d],
                {"space": t},
            )
            copy.start()
            self.third.append(copy)

    def block(self, t):
        start = pl.multiple_of(t * self.rows, self.rows)
        taps = self.got[0, :, pl.ds(start, self.rows), :]
        return taps.reshape(self.chunk * self.rows, self.inputs)

    def to_copies(self):
        total = self.block(self.me)
        for d in range(1, self.parts):
            self.third[d - 1].wait_recv()
            total = total + self.near[d - 1].astype(f32)
        self.whole[0] = total * self.scaling
        self.fourth = []
        for d in range(1, self.dp):
            copy = remote(
                self.whole.at[0],
                self.whole.at[d],
                self.sends.at[3, d],
                self.recvs.at[3, d],
                {"dp": lax.rem(self.mine + d, self.dp)},
            )
            copy.start()
            self.fourth.append(copy)

    def put(self, c, d):
        for u in range(self.chunk):
            taps = self.whole[d, u * self.rows : (u + 1) * self.rows, :]
            self.out[self.place(c * self.chunk + u)] = taps

    def finish(self):
        self.put(self.core * self.ranks + self.rest, 0)
        for d in range(1, self.dp):
            self.fourth[d - 1].wait_recv()
            other = lax.rem(self.mine + self.dp - d, self.dp)
            self.put(lax.rem(other, 2) * self.ranks + other // 2, d)
        for copy in self.first + self.second + self.third + self.fourth:
            copy.wait_send()


def place_of(tap_x):
    return lambda u: 9 * tap_x + u + 27 * (u // 9)


def kernel(dp, parts, scaling, sizes, acts_far, pre_far, w_ref, g_ref, coarse_out, fine_out, *scratch):
    coarse, fine = scratch[0], [scratch[9 * n + 9] for n in range(3)]
    share = (dp, parts, scaling)
    coarse_sum = Reduction(*share, coarse_out, lambda u: u, coarse, scratch[1:9])
    fine_sum = []
    for n in range(3):
        own = scratch[9 * n + 10 : 9 * n + 18]
        fine_sum.append(Reduction(*share, fine_out, place_of(n), fine[n], own))
    (wbuf, gbuf, halo, sends, recvs, w_full, mixing, g_send, g_turned, g_mixed, g_cells, g_rows, values, thin, frame, delta, acts, pre, loads) = scratch[36:]
    depth, across, height, channels = sizes
    half_x, half_y, half_z = depth // 2, across // 2, height // 2
    plane, small = across * height, half_y * half_z
    rows = channels // parts
    me, mine = lax.axis_index("space"), lax.axis_index("dp")
    core = lax.rem(mine, 2)
    partner = mine + 1 - 2 * core
    half = (w_ref.shape[0] + 1) // 2
    beside = me + 1 - 2 * lax.rem(me, 2)
    hello(dp, parts)
    load_pre = pltpu.make_async_copy(pre_far, pre, loads.at[0])
    load_acts = pltpu.make_async_copy(acts_far, acts, loads.at[1])
    load_pre.start()
    load_acts.start()

    count = 128 // half_y

    def pack(x, carry):
        for group in range(half_z // count):
            cells = [g_ref[x, group * count + j].astype(f32) for j in range(count)]
            g_send[x, :, group * 128 : (group + 1) * 128] = jnp.concatenate(cells, axis=1).astype(bf16)
        return carry

    lax.fori_loop(0, g_ref.shape[0], pack, 0)
    g_send[g_ref.shape[0]] = jnp.zeros((rows, small), bf16)
    pl.semaphore_wait(pltpu.get_barrier_semaphore(), parts + dp - 2)

    g_copies, w_copies, w_beside, forwards = [], [], [], []
    for d in range(1, parts):
        t = lax.rem(me + d, parts)
        mine_there = g_send.at[pl.ds(t * half_x, half_x + 1)]
        copy = remote(mine_there, gbuf.at[d - 1], sends.at[0, d], recvs.at[0, d], {"space": t})
        copy.start()
        g_copies.append(copy)
    own = w_ref.at[pl.ds(core * (half - 1), half)]
    for i in range(1, parts // 2):
        t = lax.rem(me + 2 * i, parts)
        copy = remote(own, wbuf.at[0, i, core], sends.at[1, i], recvs.at[1, i], {"space": t})
        copy.start()
        w_copies.append(copy)
    copy = remote(own, wbuf.at[1, 0, core], sends.at[2, 0], recvs.at[2, 0], {"space": beside})
    copy.start()
    w_beside.append(copy)
    upward = remote(
        acts_far.at[depth - 1],
        halo.at[0],
        sends.at[5, 0],
        recvs.at[5, 0],
        {"space": lax.rem(me + 1, parts)},
    )
    downward = remote(
        acts_far.at[0],
        halo.at[1],
        sends.at[5, 1],
        recvs.at[5, 1],
        {"space": lax.rem(me + parts - 1, parts)},
    )

    pl.when(me < parts - 1)(upward.start)
    pl.when(me > 0)(downward.start)

    at_z = lax.broadcasted_iota(jnp.int32, (half_y, half_z, channels), 1).reshape(small, channels)

    def spread(x, carry):
        values[x] = pre[x].astype(f32).reshape(half_y, 2, height, channels)
        for odd_y in (0, 1):
            pair = []
            for odd_z in (0, 1):
                cells = values[x, :, odd_y, pl.ds(odd_z, half_z, stride=2), :]
                cells = cells.reshape(small, channels)
                pair.append(jnp.where(cells > 0, cells, leak_slope * cells))
            earlier = jnp.where(at_z == 0, 0.0, pltpu.roll(pair[1], 1, 0))
            row = half_z * odd_y
            thin[x, odd_y, pl.ds(row, small), 0:channels] = earlier.astype(bf16)
            thin[x, odd_y, pl.ds(row, small), channels : 2 * channels] = pair[0].astype(bf16)
            thin[x, odd_y, pl.ds(row, small), 2 * channels :] = pair[1].astype(bf16)
        thin[x, 1, 0:half_z, :] = jnp.zeros((half_z, 3 * channels), bf16)
        return carry

    load_pre.wait()
    lax.fori_loop(0, depth, spread, 0)

    at_cell = lax.broadcasted_iota(jnp.int32, (across, height, channels), 1)
    at_cell = at_cell.reshape(plane, channels)

    def place(q, cells):
        cells = cells.astype(f32)
        inner = pl.ds(height, plane)
        earlier = jnp.where(at_cell == 0, 0.0, pltpu.roll(cells, 1, 0))
        later = jnp.where(at_cell == height - 1, 0.0, pltpu.roll(cells, plane - 1, 0))
        frame[q, inner, 0:channels] = earlier.astype(bf16)
        frame[q, inner, channels : 2 * channels] = cells.astype(bf16)
        frame[q, inner, 2 * channels :] = later.astype(bf16)
        nothing = jnp.zeros((height, 3 * channels), bf16)
        frame[q, 0:height, :] = nothing
        frame[q, pl.ds(height + plane, height), :] = nothing

    def place_own(x, carry):
        place(x + 1, acts[x])
        return carry

    load_acts.wait()
    lax.fori_loop(0, depth, place_own, 0)

    def take_cotangents(s, block):
        start = pl.multiple_of(s * rows, rows)
        g_turned[:, pl.ds(start, rows), :] = block.astype(f32)

    take_cotangents(me, g_send[pl.ds(me * half_x, half_x + 1)])
    for d in range(1, parts):
        g_copies[d - 1].wait_recv()
        take_cotangents(lax.rem(me + parts - d, parts), gbuf[d - 1])
    for p in range(half_x + 1):
        g_mixed[p] = g_turned[p].T
        for y in range(half_y):
            cells = g_mixed[p, pl.ds(y, half_z, stride=half_y), :]
            g_cells[p, y * half_z : (y + 1) * half_z, :] = cells
        g_turned[p] = g_cells[p].T

    for i in range(1, parts // 2):
        w_copies[i - 1].wait_recv()
        block = wbuf.at[0, i, core]
        copy = remote(block, wbuf.at[1, i, core], sends.at[2, i], recvs.at[2, i], {"space": beside})
        copy.start()
        w_beside.append(copy)
        copy = remote(block, block, sends.at[3, i], recvs.at[3, i], {"dp": partner})
        copy.start()
        forwards.append((0, i, copy))
    for tap_x in range(3):
        for tap_y in range(3):
            total = None
            for p in range(half_x):
                at_p, at_x = (p + 1, 2 * p + 1) if tap_x == 0 else (p, 2 * p + tap_x - 1)
                lhs = g_turned[at_p].astype(bf16)
                row = half_z if tap_y == 2 else 0
                rhs = thin[at_x, 0 if tap_y == 1 else 1, row : row + small, :]
                term = jnp.dot(lhs, rhs, preferred_element_type=f32)
                total = term if total is None else total + term
            for tap_z in range(3):
                coarse[9 * tap_x + 3 * tap_y + tap_z] = total[
                    :, tap_z * channels : (tap_z + 1) * channels
                ]
    for u in range(27, coarse.shape[0]):
        coarse[u] = jnp.zeros((channels, channels), f32)
    coarse_sum.to_core()
    for i in range(parts // 2):
        w_beside[i].wait_recv()
        block = wbuf.at[1, i, core]
        copy = remote(block, block, sends.at[4, i], recvs.at[4, i], {"dp": partner})
        copy.start()
        forwards.append((1, i, copy))
    for p in range(half_x + 1):
        cells = g_cells[p]
        later = jnp.where(at_z == half_z - 1, 0.0, pltpu.roll(cells, small - 1, 0))
        g_rows[p, 0:small, 0:channels] = cells.astype(bf16)
        g_rows[p, 0:small, channels:] = later.astype(bf16)
        g_rows[p, small : small + half_z, :] = jnp.zeros((half_z, 2 * channels), bf16)

    def take_filters(s, part, block):
        start = pl.multiple_of(s * rows, rows)
        w_full[pl.ds(part * (half - 1), half), pl.ds(start, rows), :] = block.astype(f32)

    for part in (0, 1):
        take_filters(me, part, w_ref[part * (half - 1) : part * (half - 1) + half])
    for side, i, copy in forwards:
        copy.wait_recv()
        source = beside if side else me
        for part in (0, 1):
            take_filters(lax.rem(source + parts - 2 * i, parts), part, wbuf[side, i, part])

    def mix(t, carry):
        mixing[t, 0:channels, 0:channels] = w_full[3 * t + 1].astype(bf16)
        mixing[t, 0:channels, channels:] = w_full[3 * t + 2].astype(bf16)
        mixing[t, channels:, 0:channels] = jnp.zeros((channels, channels), bf16)
        mixing[t, channels:, channels:] = w_full[3 * t].astype(bf16)
        return carry

    lax.fori_loop(0, 9, mix, 0)
    coarse_sum.to_chips()

    def propagate(p, carry):
        for odd_x in (0, 1):
            for odd_y in (0, 1):
                total = None
                for tap_x, move_x in parity_taps[odd_x]:
                    for tap_y, move_y in parity_taps[odd_y]:
                        cells = g_rows[p + move_x, move_y * half_z : move_y * half_z + small, :]
                        term = jnp.dot(
                            cells, mixing[3 * tap_x + tap_y], preferred_element_type=f32
                        )
                        total = term if total is None else total + term
                for odd_z in (0, 1):
                    where = (2 * p + odd_x, slice(None), odd_y, pl.ds(odd_z, half_z, stride=2))
                    before = values[where].reshape(small, channels)
                    piece = total[:, odd_z * channels : (odd_z + 1) * channels]
                    piece = piece * jnp.where(before > 0, 1.0, leak_slope)
                    values[where] = piece.reshape(half_y, half_z, channels)
        for odd_x in (0, 1):
            x = 2 * p + odd_x
            cells = values[x].reshape(plane, channels).astype(bf16)
            delta[pl.ds(pl.multiple_of(x * channels, channels), channels), :] = cells.T
        return carry

    lax.fori_loop(0, half_x, propagate, 0)

    for tap_x in range(3):
        for u in range(fine[tap_x].shape[0]):
            fine[tap_x][u] = jnp.zeros((channels, channels), f32)

    def layer(q):
        low, high = max(0, q - 2), min(depth - 1, q)

        slabs = [frame[q, y * height : y * height + plane, :] for y in range(3)]
        lhs = delta[low * channels : (high + 1) * channels, :]
        total = jnp.dot(lhs, jnp.concatenate(slabs, axis=1), preferred_element_type=f32)
        for x in range(low, high + 1):
            for tap in range(9):
                fine[q - x][tap] += total[
                    (x - low) * channels : (x - low + 1) * channels,
                    tap * channels : (tap + 1) * channels,
                ]

    layer(1)
    coarse_sum.to_space()
    for q in range(2, depth):
        layer(q)
    coarse_sum.to_copies()

    @pl.when(me > 0)
    def _():
        upward.wait_recv()
        place(0, halo[0])
        layer(0)

    fine_sum[0].to_core()
    layer(depth)
    fine_sum[1].to_core()
    fine_sum[0].to_chips()

    @pl.when(me < parts - 1)
    def _():
        downward.wait_recv()
        place(depth + 1, halo[1])
        layer(depth + 1)

    fine_sum[2].to_core()
    fine_sum[1].to_chips()
    fine_sum[0].to_space()
    fine_sum[2].to_chips()
    fine_sum[1].to_space()
    coarse_sum.finish()
    fine_sum[0].to_copies()
    fine_sum[2].to_space()
    fine_sum[1].to_copies()
    fine_sum[0].finish()
    fine_sum[1].finish()
    fine_sum[2].to_copies()
    fine_sum[2].finish()
    for copy in g_copies + w_copies + w_beside + [copy for _, _, copy in forwards]:
        copy.wait_send()
    pl.when(me < parts - 1)(upward.wait_send)
    pl.when(me > 0)(downward.wait_send)


def reduction_scratch(dp, parts, channels, taps):
    chunk = -(-taps // dp)
    ranks = dp // 2
    rows = channels // parts
    most = max(dp, parts)
    return [
        VMEM((chunk * dp, channels, channels), f32),
        VMEM((ranks, chunk, channels, channels), f32),
        VMEM((ranks - 1, chunk, channels, channels), bf16),
        VMEM((ranks - 1, chunk, channels, channels), bf16),
        VMEM((parts - 1, chunk * rows, channels), bf16),
        VMEM((parts - 1, chunk * rows, channels), bf16),
        VMEM((dp, chunk * rows, channels), f32),
        pltpu.SemaphoreType.DMA((4, most)),
        pltpu.SemaphoreType.DMA((4, most)),
    ]


def gradients(dp, parts, scaling, sizes, acts, pre, w, g):
    depth, across, height, channels = sizes
    half_x, half_y, half_z = depth // 2, across // 2, height // 2
    plane, small = across * height, half_y * half_z
    chunk = -(-27 // dp)
    rows = channels // parts
    half = (w.shape[0] + 1) // 2
    units = [chunk * dp, place_of(2)(-(-9 // dp) * dp - 1) + 1]
    flops = 2 * 27 * channels * channels * (depth * plane + 2 * half_x * small)
    return pl.pallas_call(
        functools.partial(kernel, dp, parts, scaling, sizes),
        out_shape=[
            jax.ShapeDtypeStruct((n, rows, channels), f32) for n in units
        ],
        in_specs=[pl.BlockSpec(memory_space=pl.ANY)] * 2 + [pl.BlockSpec(memory_space=VMEM)] * 2,
        out_specs=[pl.BlockSpec(memory_space=VMEM)] * 2,
        scratch_shapes=reduction_scratch(dp, parts, channels, 27)
        + reduction_scratch(dp, parts, channels, 9) * 3
        + [
            VMEM((2, parts // 2, 2, half, rows, channels), bf16),
            VMEM((parts - 1, half_x + 1, rows, small), bf16),
            VMEM((2, plane, channels), bf16),
            pltpu.SemaphoreType.DMA((6, parts)),
            pltpu.SemaphoreType.DMA((6, parts)),
            VMEM((27, channels, channels), f32),
            VMEM((9, 2 * channels, 2 * channels), bf16),
            VMEM((g.shape[0] + 1, rows, small), bf16),
            VMEM((half_x + 1, channels, small), f32),
            VMEM((half_x + 1, small, channels), f32),
            VMEM((half_x + 1, small, channels), f32),
            VMEM((half_x + 1, small + half_z, 2 * channels), bf16),
            VMEM((depth, half_y, 2, height, channels), f32),
            VMEM((depth, 2, small + half_z, 3 * channels), bf16),
            VMEM((depth + 2, plane + 2 * height, 3 * channels), bf16),
            VMEM((depth * channels, plane), bf16),
            VMEM((depth, plane, channels), bf16),
            VMEM((depth, plane, channels), bf16),
            pltpu.SemaphoreType.DMA((2,)),
        ],
        cost_estimate=pl.CostEstimate(flops=flops, bytes_accessed=8 << 20, transcendentals=0),
        compiler_params=pltpu.CompilerParams(
            collective_id=0, has_side_effects=True, vmem_limit_bytes=56 << 20
        ),
    )(acts, pre, w, g)


def body(acts_in, pre_act, weight_two, grad_out):
    parts = lax.axis_size("space")
    groups = lax.axis_size("dp")
    depth, across, height, channels = sizes = acts_in.shape[1:]
    rows = weight_two.shape[0]
    scaling = 1.0 / math.sqrt(groups * depth * parts * across * height)
    turned = grad_out[0].transpose(0, 2, 3, 1)
    shard = weight_two.reshape(rows, 27, channels).transpose(1, 0, 2)
    flat = (depth, across * height, channels)
    coarse, fine = gradients(
        groups, parts, scaling, sizes, acts_in.reshape(flat), pre_act.reshape(flat), shard, turned
    )

    def by_filter(totals):
        taps = totals[:27]
        return taps.transpose(1, 0, 2).reshape(rows, 3, 3, 3, channels)

    return (by_filter(fine), by_filter(coarse))


def solution(mesh):
    placed = (
        P("dp", "space", None, None, None),
        P("dp", "space", None, None, None),
        P("space", None, None, None, None),
        P("dp", None, None, None, "space"),
    )
    return jax.shard_map(
        body,
        mesh=mesh,
        in_specs=placed,
        out_specs=(P("space", None, None, None, None), P("space", None, None, None, None)),
        check_vma=False,
    )
```

```python
import functools
import math

import jax
import jax.numpy as jnp
from jax import lax
from jax.experimental import pallas as pl
from jax.experimental.pallas import tpu as pltpu
from jax.sharding import PartitionSpec as P

leak_slope = 0.3
parity_taps = {0: ((1, 0),), 1: ((0, 1), (2, 0))}
MESH = pl.DeviceIdType.MESH
VMEM = pltpu.VMEM
f32, bf16 = jnp.float32, jnp.bfloat16


def remote(src, dst, send, recv, target):
    return pltpu.make_async_remote_copy(
        src_ref=src,
        dst_ref=dst,
        send_sem=send,
        recv_sem=recv,
        device_id=target,
        device_id_type=MESH,
    )


def hello(dp, parts):
    me, mine = lax.axis_index("space"), lax.axis_index("dp")
    barrier = pltpu.get_barrier_semaphore()
    for d in range(1, parts):
        pl.semaphore_signal(
            barrier, inc=1, device_id={"space": lax.rem(me + d, parts)}, device_id_type=MESH
        )
    for d in range(1, dp):
        pl.semaphore_signal(
            barrier, inc=1, device_id={"dp": lax.rem(mine + d, dp)}, device_id_type=MESH
        )


class Reduction:
    def __init__(self, dp, parts, scaling, out, place, part, scratch):
        self.place = place
        self.dp, self.parts, self.scaling, self.out, self.part = dp, parts, scaling, out, part
        self.got, self.away, self.came, self.apart, self.near, self.whole, self.sends, self.recvs = scratch
        self.me, self.mine = lax.axis_index("space"), lax.axis_index("dp")
        self.core = lax.rem(self.mine, 2)
        self.rest = self.mine // 2
        self.ranks = dp // 2
        self.chunk = part.shape[0] // dp
        self.half = self.chunk * self.ranks
        self.order = list(range(1, self.ranks)) + [0]
        self.rows = part.shape[1] // parts
        self.inputs = part.shape[2]

    def to_core(self):
        self.first = []
        theirs = (1 - self.core) * self.half
        for d in self.order:
            j = lax.rem(self.rest + d, self.ranks)
            copy = remote(
                self.part.at[pl.ds(theirs + j * self.chunk, self.chunk)],
                self.got.at[d],
                self.sends.at[0, d],
                self.recvs.at[0, d],
                {"dp": self.mine + 1 - 2 * self.core},
            )
            copy.start()
            self.first.append(copy)

    def to_chips(self):
        self.second = []
        for d, copy in zip(self.order, self.first):
            j = lax.rem(self.rest + d, self.ranks)
            base = self.core * self.half + j * self.chunk
            copy.wait_recv()
            if d:

                def fill(u, carry):
                    self.away[d - 1, u] = (self.part[base + u] + self.got[d, u]).astype(bf16)
                    return carry

                lax.fori_loop(0, self.chunk, fill, 0)
                onward = remote(
                    self.away.at[d - 1],
                    self.came.at[d - 1],
                    self.sends.at[1, d],
                    self.recvs.at[1, d],
                    {"dp": 2 * j + self.core},
                )
                onward.start()
                self.second.append(onward)

    def to_space(self):
        base = self.core * self.half + self.rest * self.chunk
        for onward in self.second:
            onward.wait_recv()

        def settle(u, carry):
            total = self.part[base + u] + self.got[0, u]
            for d in range(1, self.ranks):
                total = total + self.came[d - 1, u].astype(f32)
            self.got[0, u] = total
            return carry

        lax.fori_loop(0, self.chunk, settle, 0)
        self.third = []
        for d in range(1, self.parts):
            t = lax.rem(self.me + d, self.parts)
            self.apart[d - 1] = self.block(t).astype(bf16)
            copy = remote(
                self.apart.at[d - 1],
                self.near.at[d - 1],
                self.sends.at[2, d],
                self.recvs.at[2, d],
                {"space": t},
            )
            copy.start()
            self.third.append(copy)

    def block(self, t):
        start = pl.multiple_of(t * self.rows, self.rows)
        taps = self.got[0, :, pl.ds(start, self.rows), :]
        return taps.reshape(self.chunk * self.rows, self.inputs)

    def to_copies(self):
        total = self.block(self.me)
        for d in range(1, self.parts):
            self.third[d - 1].wait_recv()
            total = total + self.near[d - 1].astype(f32)
        self.whole[0] = total * self.scaling
        self.fourth = []
        for d in range(1, self.dp):
            copy = remote(
                self.whole.at[0],
                self.whole.at[d],
                self.sends.at[3, d],
                self.recvs.at[3, d],
                {"dp": lax.rem(self.mine + d, self.dp)},
            )
            copy.start()
            self.fourth.append(copy)

    def put(self, c, d):
        for u in range(self.chunk):
            taps = self.whole[d, u * self.rows : (u + 1) * self.rows, :]
            self.out[self.place(c * self.chunk + u)] = taps

    def finish(self):
        self.put(self.core * self.ranks + self.rest, 0)
        for d in range(1, self.dp):
            self.fourth[d - 1].wait_recv()
            other = lax.rem(self.mine + self.dp - d, self.dp)
            self.put(lax.rem(other, 2) * self.ranks + other // 2, d)
        for copy in self.first + self.second + self.third + self.fourth:
            copy.wait_send()


def middle_place(u):
    return u + 9 + 18 * (u // 9)


def outer_place(u):
    return u + 9 * (u // 9)


def kernel(dp, parts, scaling, sizes, acts_far, pre_far, w_ref, g_ref, coarse_out, fine_out, *scratch):
    coarse, middle, outer = scratch[0], scratch[9], scratch[18]
    share = (dp, parts, scaling)
    coarse_sum = Reduction(*share, coarse_out, lambda u: u, coarse, scratch[1:9])
    middle_sum = Reduction(*share, fine_out, middle_place, middle, scratch[10:18])
    outer_sum = Reduction(*share, fine_out, outer_place, outer, scratch[19:27])
    (wbuf, gbuf, halo, sends, recvs, w_full, mixing, g_send, g_turned, g_mixed, g_cells, g_rows, values, thin, frame, delta, acts, pre, loads) = scratch[27:]
    depth, across, height, channels = sizes
    half_x, half_y, half_z = depth // 2, across // 2, height // 2
    plane, small = across * height, half_y * half_z
    rows = channels // parts
    me, mine = lax.axis_index("space"), lax.axis_index("dp")
    core = lax.rem(mine, 2)
    partner = mine + 1 - 2 * core
    half = (w_ref.shape[0] + 1) // 2
    beside = me + 1 - 2 * lax.rem(me, 2)
    hello(dp, parts)
    load_pre = pltpu.make_async_copy(pre_far, pre, loads.at[0])
    load_acts = pltpu.make_async_copy(acts_far, acts, loads.at[1])
    load_pre.start()
    load_acts.start()

    count = 128 // half_y

    def pack(x, carry):
        for group in range(half_z // count):
            cells = [g_ref[x, group * count + j].astype(f32) for j in range(count)]
            g_send[x, :, group * 128 : (group + 1) * 128] = jnp.concatenate(cells, axis=1).astype(bf16)
        return carry

    lax.fori_loop(0, g_ref.shape[0], pack, 0)
    g_send[g_ref.shape[0]] = jnp.zeros((rows, small), bf16)
    pl.semaphore_wait(pltpu.get_barrier_semaphore(), parts + dp - 2)

    g_copies, w_copies, w_beside, forwards = [], [], [], []
    for d in range(1, parts):
        t = lax.rem(me + d, parts)
        mine_there = g_send.at[pl.ds(t * half_x, half_x + 1)]
        copy = remote(mine_there, gbuf.at[d - 1], sends.at[0, d], recvs.at[0, d], {"space": t})
        copy.start()
        g_copies.append(copy)
    own = w_ref.at[pl.ds(core * (half - 1), half)]
    for i in range(1, parts // 2):
        t = lax.rem(me + 2 * i, parts)
        copy = remote(own, wbuf.at[0, i, core], sends.at[1, i], recvs.at[1, i], {"space": t})
        copy.start()
        w_copies.append(copy)
    copy = remote(own, wbuf.at[1, 0, core], sends.at[2, 0], recvs.at[2, 0], {"space": beside})
    copy.start()
    w_beside.append(copy)
    upward = remote(
        acts_far.at[depth - 1],
        halo.at[0],
        sends.at[5, 0],
        recvs.at[5, 0],
        {"space": lax.rem(me + 1, parts)},
    )
    downward = remote(
        acts_far.at[0],
        halo.at[1],
        sends.at[5, 1],
        recvs.at[5, 1],
        {"space": lax.rem(me + parts - 1, parts)},
    )

    at_z = lax.broadcasted_iota(jnp.int32, (half_y, half_z, channels), 1).reshape(small, channels)

    def spread(x, carry):
        values[x] = pre[x].astype(f32).reshape(half_y, 2, height, channels)
        for odd_y in (0, 1):
            pair = []
            for odd_z in (0, 1):
                cells = values[x, :, odd_y, pl.ds(odd_z, half_z, stride=2), :]
                cells = cells.reshape(small, channels)
                pair.append(jnp.where(cells > 0, cells, leak_slope * cells))
            earlier = jnp.where(at_z == 0, 0.0, pltpu.roll(pair[1], 1, 0))
            row = half_z * odd_y
            thin[x, odd_y, pl.ds(row, small), 0:channels] = earlier.astype(bf16)
            thin[x, odd_y, pl.ds(row, small), channels : 2 * channels] = pair[0].astype(bf16)
            thin[x, odd_y, pl.ds(row, small), 2 * channels :] = pair[1].astype(bf16)
        thin[x, 1, 0:half_z, :] = jnp.zeros((half_z, 3 * channels), bf16)
        return carry

    load_pre.wait()
    lax.fori_loop(0, depth, spread, 0)

    at_cell = lax.broadcasted_iota(jnp.int32, (across, height, channels), 1)
    at_cell = at_cell.reshape(plane, channels)

    def place(q, cells):
        cells = cells.astype(f32)
        inner = pl.ds(height, plane)
        earlier = jnp.where(at_cell == 0, 0.0, pltpu.roll(cells, 1, 0))
        later = jnp.where(at_cell == height - 1, 0.0, pltpu.roll(cells, plane - 1, 0))
        frame[q, inner, 0:channels] = earlier.astype(bf16)
        frame[q, inner, channels : 2 * channels] = cells.astype(bf16)
        frame[q, inner, 2 * channels :] = later.astype(bf16)
        nothing = jnp.zeros((height, 3 * channels), bf16)
        frame[q, 0:height, :] = nothing
        frame[q, pl.ds(height + plane, height), :] = nothing

    def place_own(x, carry):
        place(x + 1, acts[x])
        return carry

    load_acts.wait()
    lax.fori_loop(0, depth, place_own, 0)

    def take_cotangents(s, block):
        start = pl.multiple_of(s * rows, rows)
        g_turned[:, pl.ds(start, rows), :] = block.astype(f32)

    take_cotangents(me, g_send[pl.ds(me * half_x, half_x + 1)])
    for d in range(1, parts):
        g_copies[d - 1].wait_recv()
        take_cotangents(lax.rem(me + parts - d, parts), gbuf[d - 1])
    pl.when(me < parts - 1)(upward.start)
    pl.when(me > 0)(downward.start)
    for p in range(half_x + 1):
        g_mixed[p] = g_turned[p].T
        for y in range(half_y):
            cells = g_mixed[p, pl.ds(y, half_z, stride=half_y), :]
            g_cells[p, y * half_z : (y + 1) * half_z, :] = cells
        g_turned[p] = g_cells[p].T

    for i in range(1, parts // 2):
        w_copies[i - 1].wait_recv()
        block = wbuf.at[0, i, core]
        copy = remote(block, wbuf.at[1, i, core], sends.at[2, i], recvs.at[2, i], {"space": beside})
        copy.start()
        w_beside.append(copy)
        copy = remote(block, block, sends.at[3, i], recvs.at[3, i], {"dp": partner})
        copy.start()
        forwards.append((0, i, copy))
    for tap_x in range(3):
        for tap_y in range(3):
            total = None
            for p in range(half_x):
                at_p, at_x = (p + 1, 2 * p + 1) if tap_x == 0 else (p, 2 * p + tap_x - 1)
                lhs = g_turned[at_p].astype(bf16)
                row = half_z if tap_y == 2 else 0
                rhs = thin[at_x, 0 if tap_y == 1 else 1, row : row + small, :]
                term = jnp.dot(lhs, rhs, preferred_element_type=f32)
                total = term if total is None else total + term
            for tap_z in range(3):
                coarse[9 * tap_x + 3 * tap_y + tap_z] = total[
                    :, tap_z * channels : (tap_z + 1) * channels
                ]
    for u in range(27, coarse.shape[0]):
        coarse[u] = jnp.zeros((channels, channels), f32)
    coarse_sum.to_core()
    for i in range(parts // 2):
        w_beside[i].wait_recv()
        block = wbuf.at[1, i, core]
        copy = remote(block, block, sends.at[4, i], recvs.at[4, i], {"dp": partner})
        copy.start()
        forwards.append((1, i, copy))
    for p in range(half_x + 1):
        cells = g_cells[p]
        later = jnp.where(at_z == half_z - 1, 0.0, pltpu.roll(cells, small - 1, 0))
        g_rows[p, 0:small, 0:channels] = cells.astype(bf16)
        g_rows[p, 0:small, channels:] = later.astype(bf16)
        g_rows[p, small : small + half_z, :] = jnp.zeros((half_z, 2 * channels), bf16)

    def take_filters(s, part, block):
        start = pl.multiple_of(s * rows, rows)
        w_full[pl.ds(part * (half - 1), half), pl.ds(start, rows), :] = block.astype(f32)

    for part in (0, 1):
        take_filters(me, part, w_ref[part * (half - 1) : part * (half - 1) + half])
    for side, i, copy in forwards:
        copy.wait_recv()
        source = beside if side else me
        for part in (0, 1):
            take_filters(lax.rem(source + parts - 2 * i, parts), part, wbuf[side, i, part])

    def mix(t, carry):
        mixing[t, 0:channels, 0:channels] = w_full[3 * t + 1].astype(bf16)
        mixing[t, 0:channels, channels:] = w_full[3 * t + 2].astype(bf16)
        mixing[t, channels:, 0:channels] = jnp.zeros((channels, channels), bf16)
        mixing[t, channels:, channels:] = w_full[3 * t].astype(bf16)
        return carry

    lax.fori_loop(0, 9, mix, 0)
    coarse_sum.to_chips()

    def propagate(p, carry):
        for odd_x in (0, 1):
            for odd_y in (0, 1):
                total = None
                for tap_x, move_x in parity_taps[odd_x]:
                    for tap_y, move_y in parity_taps[odd_y]:
                        cells = g_rows[p + move_x, move_y * half_z : move_y * half_z + small, :]
                        term = jnp.dot(
                            cells, mixing[3 * tap_x + tap_y], preferred_element_type=f32
                        )
                        total = term if total is None else total + term
                for odd_z in (0, 1):
                    where = (2 * p + odd_x, slice(None), odd_y, pl.ds(odd_z, half_z, stride=2))
                    before = values[where].reshape(small, channels)
                    piece = total[:, odd_z * channels : (odd_z + 1) * channels]
                    piece = piece * jnp.where(before > 0, 1.0, leak_slope)
                    values[where] = piece.reshape(half_y, half_z, channels)
        for odd_x in (0, 1):
            x = 2 * p + odd_x
            cells = values[x].reshape(plane, channels).astype(bf16)
            delta[pl.ds(pl.multiple_of(x * channels, channels), channels), :] = cells.T
        return carry

    lax.fori_loop(0, half_x, propagate, 0)

    def clear(u, carry):
        outer[u] = jnp.zeros((channels, channels), f32)
        return carry

    lax.fori_loop(0, outer.shape[0], clear, 0)
    for u in range(middle.shape[0]):
        middle[u] = jnp.zeros((channels, channels), f32)

    def layer(q):
        low, high = max(0, q - 2), min(depth - 1, q)

        slabs = [frame[q, y * height : y * height + plane, :] for y in range(3)]
        lhs = delta[low * channels : (high + 1) * channels, :]
        total = jnp.dot(lhs, jnp.concatenate(slabs, axis=1), preferred_element_type=f32)
        for x in range(low, high + 1):
            into, first = (middle, 0) if q - x == 1 else (outer, 9 * ((q - x) // 2))
            for tap in range(9):
                into[first + tap] += total[
                    (x - low) * channels : (x - low + 1) * channels,
                    tap * channels : (tap + 1) * channels,
                ]

    layer(1)
    coarse_sum.to_space()
    for q in range(2, depth):
        layer(q)
    coarse_sum.to_copies()
    layer(depth)

    middle_sum.to_core()

    @pl.when(me > 0)
    def _():
        upward.wait_recv()
        place(0, halo[0])
        layer(0)

    middle_sum.to_chips()

    @pl.when(me < parts - 1)
    def _():
        downward.wait_recv()
        place(depth + 1, halo[1])
        layer(depth + 1)

    outer_sum.to_core()
    middle_sum.to_space()
    outer_sum.to_chips()
    coarse_sum.finish()
    middle_sum.to_copies()
    outer_sum.to_space()
    middle_sum.finish()
    outer_sum.to_copies()
    outer_sum.finish()
    for copy in g_copies + w_copies + w_beside + [copy for _, _, copy in forwards]:
        copy.wait_send()
    pl.when(me < parts - 1)(upward.wait_send)
    pl.when(me > 0)(downward.wait_send)


def reduction_scratch(dp, parts, channels, taps):
    chunk = -(-taps // dp)
    ranks = dp // 2
    rows = channels // parts
    most = max(dp, parts)
    return [
        VMEM((chunk * dp, channels, channels), f32),
        VMEM((ranks, chunk, channels, channels), f32),
        VMEM((ranks - 1, chunk, channels, channels), bf16),
        VMEM((ranks - 1, chunk, channels, channels), bf16),
        VMEM((parts - 1, chunk * rows, channels), bf16),
        VMEM((parts - 1, chunk * rows, channels), bf16),
        VMEM((dp, chunk * rows, channels), f32),
        pltpu.SemaphoreType.DMA((4, most)),
        pltpu.SemaphoreType.DMA((4, most)),
    ]


def gradients(dp, parts, scaling, sizes, acts, pre, w, g):
    depth, across, height, channels = sizes
    half_x, half_y, half_z = depth // 2, across // 2, height // 2
    plane, small = across * height, half_y * half_z
    chunk = -(-27 // dp)
    rows = channels // parts
    half = (w.shape[0] + 1) // 2
    units = [chunk * dp]
    for taps, where in ((9, middle_place), (18, outer_place)):
        units.append(where(-(-taps // dp) * dp - 1) + 1)
    flops = 2 * 27 * channels * channels * (depth * plane + 2 * half_x * small)
    return pl.pallas_call(
        functools.partial(kernel, dp, parts, scaling, sizes),
        out_shape=[
            jax.ShapeDtypeStruct((n, rows, channels), f32) for n in (units[0], max(units[1:]))
        ],
        in_specs=[pl.BlockSpec(memory_space=pl.ANY)] * 2 + [pl.BlockSpec(memory_space=VMEM)] * 2,
        out_specs=[pl.BlockSpec(memory_space=VMEM)] * 2,
        scratch_shapes=reduction_scratch(dp, parts, channels, 27)
        + reduction_scratch(dp, parts, channels, 9)
        + reduction_scratch(dp, parts, channels, 18)
        + [
            VMEM((2, parts // 2, 2, half, rows, channels), bf16),
            VMEM((parts - 1, half_x + 1, rows, small), bf16),
            VMEM((2, plane, channels), bf16),
            pltpu.SemaphoreType.DMA((6, parts)),
            pltpu.SemaphoreType.DMA((6, parts)),
            VMEM((27, channels, channels), f32),
            VMEM((9, 2 * channels, 2 * channels), bf16),
            VMEM((g.shape[0] + 1, rows, small), bf16),
            VMEM((half_x + 1, channels, small), f32),
            VMEM((half_x + 1, small, channels), f32),
            VMEM((half_x + 1, small, channels), f32),
            VMEM((half_x + 1, small + half_z, 2 * channels), bf16),
            VMEM((depth, half_y, 2, height, channels), f32),
            VMEM((depth, 2, small + half_z, 3 * channels), bf16),
            VMEM((depth + 2, plane + 2 * height, 3 * channels), bf16),
            VMEM((depth * channels, plane), bf16),
            VMEM((depth, plane, channels), bf16),
            VMEM((depth, plane, channels), bf16),
            pltpu.SemaphoreType.DMA((2,)),
        ],
        cost_estimate=pl.CostEstimate(flops=flops, bytes_accessed=8 << 20, transcendentals=0),
        compiler_params=pltpu.CompilerParams(
            collective_id=0, has_side_effects=True, vmem_limit_bytes=56 << 20
        ),
    )(acts, pre, w, g)


def body(acts_in, pre_act, weight_two, grad_out):
    parts = lax.axis_size("space")
    groups = lax.axis_size("dp")
    depth, across, height, channels = sizes = acts_in.shape[1:]
    rows = weight_two.shape[0]
    scaling = 1.0 / math.sqrt(groups * depth * parts * across * height)
    turned = grad_out[0].transpose(0, 2, 3, 1)
    shard = weight_two.reshape(rows, 27, channels).transpose(1, 0, 2)
    flat = (depth, across * height, channels)
    coarse, fine = gradients(
        groups, parts, scaling, sizes, acts_in.reshape(flat), pre_act.reshape(flat), shard, turned
    )

    def by_filter(totals):
        taps = totals[:27]
        return taps.transpose(1, 0, 2).reshape(rows, 3, 3, 3, channels)

    return (by_filter(fine), by_filter(coarse))


def solution(mesh):
    placed = (
        P("dp", "space", None, None, None),
        P("dp", "space", None, None, None),
        P("space", None, None, None, None),
        P("dp", None, None, None, "space"),
    )
    return jax.shard_map(
        body,
        mesh=mesh,
        in_specs=placed,
        out_specs=(P("space", None, None, None, None), P("space", None, None, None, None)),
        check_vma=False,
    )
```
